512 devices in a mesh: row: 64 (over y, z), col: 8 (over x, core).
Axes of the slice: x: 4, y: 8, z: 8, core: 2. Of those that a mesh axis runs over, the one named last changes fastest.
Arguments:
- vectors: bfloat16 [65536, 512], P(('row', 'col')), may hold values from -6 to 6
- onsite: float32 [65536], P(('row', 'col')), may hold values from 2.5 to 8
- tile_values: bfloat16 [64, 8, 24, 128, 128], P('row', 'col'), may hold values from -0.21875 to 0.21875
- tile_rows: int32 [64, 8, 24], P('row', 'col'), may hold values from 0 to 7
- tile_cols: int32 [64, 8, 24], P('row', 'col'), may hold values from 0 to 63
- tile_count: int32 [64, 8], P('row', 'col'), may hold values from 1 to 24, as said below
Outputs:
- states: float32 [65536, 512], P(('row', 'col'))
- upper: float32 [512, 512], replicated
The draws below stay inside these ranges and needn't reach their ends.
Inputs may be any that keep to these rules, and one draw needn't show every extreme that they name: `tile_count`: some device has all 24 slots live in every draw.
All inputs are finite; a program needn't handle non-finite values.
Results may differ from the reference program's by a relative error of at most 0.0003.
Values may be sent and summed in bfloat16 or wider, within the bound.
No kernel may reach another device: no remote copies, remote signals or barrier semaphores. Data moves between devices by JAX's collectives and lax.ppermute only.
A program may use at most 128 MiB of HBM per device.

```python
import math
import jax
import jax.numpy as jnp
from jax import lax

B = 128
K = 512
BD = 1
TILES = 24
RB = 8
CB = 64
M = 65536
N_ROW = 64
N_COL = 8


def draw_tile_count(key, part):
    key = jax.random.fold_in(key, 5)
    first, second = jax.random.split(key)
    divisor = jax.random.randint(first, (N_ROW * N_COL,), 1, 5)
    counts = jnp.maximum(TILES // divisor, 1).astype(jnp.int32)
    busiest = jax.random.randint(second, (), 0, N_ROW * N_COL)
    counts = counts.at[busiest].set(TILES)
    return counts.reshape(N_ROW, N_COL).astype(jnp.int32)


def place_ends(drawn, rng, least, top_value):
    longest = drawn.shape.index(max(drawn.shape))
    spots = []
    for shift in (0, 1):
        where = [jax.random.randint(jax.random.fold_in(rng, axis), (), 0, length) for axis, length in enumerate(drawn.shape)]
        where[longest] = (where[longest] + shift) % drawn.shape[longest]
        spots.append(tuple(where))
    return drawn.at[spots[0]].set(least).at[spots[1]].set(top_value)


def steps_of(own_key, extent, cuts, low, top_value):
    level = 1.0
    for axis_at, shards_of in cuts:
        heights = jax.random.uniform(jax.random.fold_in(jax.random.fold_in(own_key, 6), axis_at), (shards_of,), jnp.float32, low / len(cuts), top_value / len(cuts))
        level = level * jnp.repeat(jnp.exp(heights), extent[axis_at] // shards_of).reshape((-1,) + (1,) * (len(extent) - 1 - axis_at))
    return level


def normal_values(key, dims, deviation, most, cuts=(), kind=jnp.bfloat16):
    level = steps_of(key, dims, cuts, -0.22, 0.18) if cuts else 1.0
    result = jax.random.normal(key, dims, jnp.float32) * deviation * level
    return jnp.minimum(jnp.maximum(result, -most), most).astype(kind)


def setup_inputs(seed: int = 0) -> dict:
    key_list = jax.random.split(jax.random.key(seed), 7)
    vectors = normal_values(key_list[0], (M, K), 1.0, 6.0, ((0, 512),))
    onsite = jnp.clip(jnp.exp(math.log(8.0) - 1.1631508 * jax.random.uniform(key_list[1], (M,), jnp.float32) ** steps_of(key_list[1], (M,), ((0, 512),), -0.2, 0.2)), 2.5, 8.0)
    tile_values = normal_values(key_list[2], (N_ROW, N_COL, TILES, B, B), (2 * B * TILES // RB) ** -0.5, 0.21875, ((0, 64), (1, 8)))
    tile_rows = place_ends(jax.random.randint(key_list[3], (N_ROW, N_COL, TILES), 0, RB), jax.random.fold_in(key_list[3], 1), 0, RB - 1).astype(jnp.int32)
    tile_cols = place_ends(jax.random.randint(key_list[4], (N_ROW, N_COL, TILES), 0, CB), jax.random.fold_in(key_list[4], 1), 0, CB - 1).astype(jnp.int32)
    tile_count = draw_tile_count(jax.random.fold_in(key_list[6], 71), 0)
    return dict(vectors=vectors, onsite=onsite, tile_values=tile_values, tile_rows=tile_rows, tile_cols=tile_cols, tile_count=tile_count)


def reference(vectors, onsite, tile_values, tile_rows, tile_cols, tile_count):
    nrow = tile_count.shape[0]
    ncol = tile_count.shape[1]
    width = tile_values.shape[-1]
    kstates = vectors.shape[1]
    slots = tile_values.shape[2]
    rblocks = ncol * BD
    blocks = vectors.reshape(-1, width, kstates)

    def one_device(acc, index):
        r = index // ncol
        c = index % ncol
        tiles = tile_values[r, c].astype(jnp.float32)
        rows_here = tile_rows[r, c]
        cols_here = tile_cols[r, c]
        glob = (cols_here // BD * rblocks + c * BD + cols_here % BD).astype(jnp.int32)
        picked = jnp.take(blocks, glob, axis=0).astype(jnp.float32)
        prod = jnp.einsum('tij,tjk->tik', tiles, picked)
        live = (jnp.arange(slots) < tile_count[r, c]).astype(jnp.float32)
        place = (rows_here[None, :] == jnp.arange(rblocks)[:, None]).astype(jnp.float32) * live[None, :]
        contrib = jnp.einsum('bt,tik->bik', place, prod, precision=lax.Precision.HIGHEST)
        start = (r * rblocks).astype(jnp.int32)
        old = lax.dynamic_slice_in_dim(acc, start, rblocks, 0)
        return (lax.dynamic_update_slice_in_dim(acc, old + contrib, start, 0), None)
    acc = jnp.zeros((nrow * rblocks, width, kstates), jnp.float32)
    acc, _ = lax.scan(one_device, acc, jnp.arange(nrow * ncol, dtype=jnp.int32))
    applied = acc.reshape(-1, kstates) + onsite[:, None] * vectors.astype(jnp.float32)
    gram = jnp.dot(applied.T, applied, precision=lax.Precision.HIGHEST)
    upper = jnp.linalg.cholesky(gram).T
    inverse = jax.scipy.linalg.solve_triangular(upper, jnp.eye(kstates, dtype=jnp.float32), lower=False)
    states = jnp.dot(applied, inverse, precision=lax.Precision.HIGHEST)
    return (states, upper)
```

```python
import functools

import jax
import jax.numpy as jnp
from jax import lax
from jax.experimental import pallas as pl
from jax.experimental.pallas import tpu as pltpu
from jax.sharding import Mesh, PartitionSpec as P

FULL = lax.Precision.HIGHEST
STRIP = 8


def dot_full(left, right, left_dim, right_dim):
    dims = (((left_dim,), (right_dim,)), ((), ()))
    return lax.dot_general(left, right, dims, precision=FULL, preferred_element_type=jnp.float32)


def tile_products(kcore_ref, rows_ref, cols_ref, count_ref, tiles_ref, blocks_ref, keep_ref, send_ref, held, sems):
    slots = tiles_ref.shape[0]
    count = count_ref[0]
    kcore = kcore_ref[0]

    def fetch(t):
        return pltpu.make_async_copy(blocks_ref.at[cols_ref[t]], held.at[t], sems.at[t])

    for t in range(slots):
        @pl.when(t < count)
        def _():
            fetch(t).start()

    keep_ref[...] = jnp.zeros_like(keep_ref)
    send_ref[...] = jnp.zeros_like(send_ref)

    @pl.loop(0, count)
    def _(t):
        fetch(t).wait()
        row = rows_ref[t]
        prod = jnp.dot(tiles_ref[t], held[t], preferred_element_type=jnp.float32)
        own = lax.rem(row, 2) == kcore

        @pl.when(own)
        def _():
            keep_ref[row // 2] += prod

        @pl.when(jnp.logical_not(own))
        def _():
            send_ref[row // 2] += prod


def gram_blocks(parts_ref, local_ref, applied_ref, gram_ref):
    width = gram_ref.shape[1]
    applied = local_ref[...]
    for i in range(parts_ref.shape[0]):
        applied = applied + parts_ref[i]
    applied_ref[...] = applied
    nblocks = applied.shape[1] // width
    at = 0
    for j in range(nblocks):
        row = dot_full(applied[:, j * width:(j + 1) * width], applied[:, j * width:], 0, 0)
        for k in range(nblocks - j):
            gram_ref[at] = row[:, k * width:(k + 1) * width]
            at += 1


def factor_diagonal(a_ref, inverse_ref, u_ref, base, n):
    sub = lax.broadcasted_iota(jnp.int32, (STRIP, n), 0)
    lane = lax.broadcasted_iota(jnp.int32, (STRIP, n), 1)
    strips = n // STRIP

    def spread(rows, k):
        return jnp.broadcast_to(rows[k:k + 1, :], (STRIP, n))

    rows_a = [a_ref[STRIP * i:STRIP * (i + 1), :] for i in range(strips)]
    rows_e = [jnp.where(lane == sub + STRIP * i, 1.0, 0.0) for i in range(strips)]
    for s in range(strips):
        first = STRIP * s
        here = slice(first, first + STRIP)
        cols = [jnp.broadcast_to(rows_a[s][:, first + k:first + k + 1], (STRIP, n)) for k in range(STRIP)]
        down_a, down_e = rows_a[s], rows_e[s]
        full_a, full_e = rows_a[s], rows_e[s]
        pivots = None
        for k in range(STRIP):
            pivot = spread(cols[k], k)
            recip = 1.0 / pivot
            ratio = cols[k] * recip
            at = sub == k
            both = jnp.where(at, -recip, ratio)
            below = jnp.where(sub > k, ratio, 0.0)
            for b in range(k + 1, STRIP):
                cols[b] = jnp.where(at, 0.0, cols[b]) - both * spread(cols[b], k)
            row_a, row_e = spread(full_a, k), spread(full_e, k)
            down_a = down_a - below * spread(down_a, k)
            down_e = down_e - below * spread(down_e, k)
            full_a = jnp.where(at, 0.0, full_a) - both * row_a
            full_e = jnp.where(at, 0.0, full_e) - both * row_e
            pivots = pivot if pivots is None else jnp.where(sub >= k, pivot, pivots)
        scale = lax.rsqrt(pivots)
        u_ref[base + first:base + first + STRIP, base:base + n] = jnp.where(lane >= sub + first, down_a * scale, 0.0)
        inverse_ref[here, :] = down_e * scale
        spread_a = [spread(full_a, k) for k in range(STRIP)]
        spread_e = [spread(full_e, k) for k in range(STRIP)]
        for i in range(s + 1, strips):
            next_a, next_e = rows_a[i], rows_e[i]
            for k in range(STRIP):
                c = jnp.broadcast_to(rows_a[i][:, first + k:first + k + 1], (STRIP, n))
                next_a = next_a - c * spread_a[k]
                next_e = next_e - c * spread_e[k]
            rows_a[i], rows_e[i] = next_a, next_e


def factor_and_solve(gram_ref, applied_ref, states_ref, u_ref, work, inverse):
    n = gram_ref.shape[1]
    size = u_ref.shape[0]
    nblocks = size // n
    at = 0
    for j in range(nblocks):
        for k in range(j, nblocks):
            work[n * j:n * (j + 1), n * k:n * (k + 1)] = gram_ref[at]
            at += 1
    states_ref[...] = applied_ref[...]
    u_ref[...] = jnp.zeros_like(u_ref)
    for j in range(nblocks):
        lo, hi = n * j, n * (j + 1)
        factor_diagonal(work.at[lo:hi, lo:hi], inverse, u_ref, lo, n)
        inv = inverse[...]
        solved = dot_full(states_ref[:, lo:hi], inv, 1, 1)
        states_ref[:, lo:hi] = solved
        if hi < size:
            panel = dot_full(inv, work[lo:hi, hi:], 1, 0)
            u_ref[lo:hi, hi:] = panel
            for k in range(j + 1, nblocks):
                a, b = n * k, n * (k + 1)
                work[a:b, a:] -= dot_full(panel[:, a - hi:b - hi], panel[:, a - hi:], 0, 0)
            states_ref[:, hi:] -= dot_full(solved, panel, 1, 0)


def call(body, outs, in_spaces, scratch=(), mib=40):
    return pl.pallas_call(
        body,
        out_shape=outs,
        in_specs=[pl.BlockSpec(memory_space=space) for space in in_spaces],
        out_specs=[pl.BlockSpec(memory_space=pltpu.VMEM) for _ in outs],
        scratch_shapes=list(scratch),
        compiler_params=pltpu.CompilerParams(vmem_limit_bytes=mib * 2**20),
    )


def per_device(vectors, onsite, tile_values, tile_rows, tile_cols, tile_count):
    own_rows, kstates = vectors.shape
    width = tile_values.shape[-1]
    slots = tile_values.shape[2]
    f32 = jnp.float32
    vm, sm, anywhere = pltpu.VMEM, pltpu.SMEM, pl.ANY
    halves = lax.axis_size("x")
    kcore = lax.axis_index("k").astype(jnp.int32).reshape(1)

    gathered = lax.all_gather(vectors, ("y", "z"), axis=0, tiled=True).reshape(-1, width, kstates)
    local = onsite[:, None] * vectors.astype(f32)

    part = jax.ShapeDtypeStruct((halves, width, kstates), f32)
    keep, send = call(
        tile_products,
        [part, part],
        [sm, sm, sm, sm, vm, anywhere],
        [vm((slots, width, kstates), jnp.bfloat16), pltpu.SemaphoreType.DMA((slots,))],
    )(kcore, tile_rows.reshape(slots), tile_cols.reshape(slots), tile_count.reshape(1), tile_values[0, 0], gathered)
    other = lax.ppermute(send, "k", [(0, 1), (1, 0)])
    parts = lax.all_to_all(keep + other, "x", 0, 0, tiled=True)

    nblocks = kstates // width
    upper_blocks = nblocks * (nblocks + 1) // 2
    applied, gram = call(
        gram_blocks,
        [jax.ShapeDtypeStruct((own_rows, kstates), f32), jax.ShapeDtypeStruct((upper_blocks, width, width), f32)],
        [vm, vm],
    )(parts, local)

    ncol = lax.axis_size(("x", "k"))
    nrow = lax.axis_size(("y", "z"))
    piece = lax.all_to_all(gram.reshape(ncol, -1, width), ("x", "k"), 0, 0, tiled=True).sum(0)
    shape = piece.shape
    piece = lax.all_to_all(piece.reshape(nrow, -1), ("y", "z"), 0, 0, tiled=True).sum(0, keepdims=True)
    piece = lax.all_to_all(jnp.tile(piece, (nrow, 1)), ("y", "z"), 0, 0, tiled=True).reshape(shape)
    gram = lax.all_to_all(jnp.tile(piece[None], (ncol, 1, 1)), ("x", "k"), 0, 0, tiled=True)
    gram = gram.reshape(upper_blocks, width, width)

    states, upper = call(
        factor_and_solve,
        [jax.ShapeDtypeStruct((own_rows, kstates), f32), jax.ShapeDtypeStruct((kstates, kstates), f32)],
        [vm, vm],
        [vm((kstates, kstates), f32), vm((width, width), f32)],
    )(gram, applied)
    return (states, upper)


def solution(mesh):
    fine = Mesh(mesh.devices.reshape(8, 8, 4, 2), ("y", "z", "x", "k"))
    row, col = ("y", "z"), ("x", "k")
    return jax.shard_map(
        per_device,
        mesh=fine,
        in_specs=(
            P(row + col, None),
            P(row + col),
            P(row, col, None, None, None),
            P(row, col, None),
            P(row, col, None),
            P(row, col),
        ),
        out_specs=(P(row + col, None), P()),
        check_vma=False,
    )
```

```python
import functools

import jax
import jax.numpy as jnp
from jax import lax
from jax.experimental import pallas as pl
from jax.experimental.pallas import tpu as pltpu
from jax.sharding import Mesh, PartitionSpec as P

FULL = lax.Precision.HIGHEST
STRIP = 8
GROUP = 3


def dot_full(left, right, left_dim, right_dim):
    dims = (((left_dim,), (right_dim,)), ((), ()))
    return lax.dot_general(left, right, dims, precision=FULL, preferred_element_type=jnp.float32)


def tile_products(meta_ref, tiles_ref, *refs):
    *sources, keep_ref, send_ref, sums, tiles, held, tile_sem, sems, out_sems = refs
    slots = tiles_ref.shape[0]
    per_core = keep_ref.shape[0]
    count = meta_ref[3 * slots]
    steps = (count + GROUP - 1) // GROUP

    fetch_tiles = pltpu.make_async_copy(tiles_ref, tiles, tile_sem)
    fetch_tiles.start()

    @pl.loop(0, steps * GROUP)
    def _(t):
        for at, source in enumerate(sources):
            @pl.when(meta_ref[slots + t] == at)
            def _():
                pltpu.make_async_copy(source.at[meta_ref[2 * slots + t]], held.at[t], sems.at[t]).start()

    sums[...] = jnp.zeros_like(sums)
    fetch_tiles.wait()

    @pl.loop(0, steps)
    def _(step):
        first = step * GROUP
        prods = []
        for t in range(GROUP):
            pltpu.make_async_copy(sources[0].at[0], held.at[first + t], sems.at[first + t]).wait()
            tile = tiles[first + t]
            tile = jnp.where(first + t < count, tile, jnp.zeros_like(tile))
            prods.append(jnp.dot(tile, held[first + t], preferred_element_type=jnp.float32))
        for t in range(GROUP):
            sums[meta_ref[first + t]] += prods[t]

    put_keep = pltpu.make_async_copy(sums.at[:per_core], keep_ref, out_sems.at[0])
    put_send = pltpu.make_async_copy(sums.at[per_core:], send_ref, out_sems.at[1])
    put_send.start()
    put_keep.start()
    put_send.wait()
    put_keep.wait()


def gram_blocks(parts_ref, local_ref, applied_ref, gram_ref):
    width = gram_ref.shape[1]
    applied = local_ref[...]
    for i in range(parts_ref.shape[0]):
        applied = applied + parts_ref[i]
    applied_ref[...] = applied
    nblocks = applied.shape[1] // width
    at = 0
    for j in range(nblocks):
        row = dot_full(applied[:, j * width:(j + 1) * width], applied[:, j * width:], 0, 0)
        for k in range(nblocks - j):
            gram_ref[at] = row[:, k * width:(k + 1) * width]
            at += 1


def factor_diagonal(a_ref, inverse_ref, u_ref, base, n):
    sub = lax.broadcasted_iota(jnp.int32, (STRIP, n), 0)
    lane = lax.broadcasted_iota(jnp.int32, (STRIP, n), 1)
    strips = n // STRIP

    def spread(rows, k):
        return jnp.broadcast_to(rows[k:k + 1, :], (STRIP, n))

    rows_a = [a_ref[STRIP * i:STRIP * (i + 1), :] for i in range(strips)]
    rows_e = [jnp.where(lane == sub + STRIP * i, 1.0, 0.0) for i in range(strips)]
    for s in range(strips):
        first = STRIP * s
        here = slice(first, first + STRIP)
        cols = [jnp.broadcast_to(rows_a[s][:, first + k:first + k + 1], (STRIP, n)) for k in range(STRIP)]
        down_a, down_e = rows_a[s], rows_e[s]
        full_a, full_e = rows_a[s], rows_e[s]
        pivots = None
        for k in range(STRIP):
            pivot = spread(cols[k], k)
            recip = 1.0 / pivot
            ratio = cols[k] * recip
            at = sub == k
            both = jnp.where(at, -recip, ratio)
            below = jnp.where(sub > k, ratio, 0.0)
            for b in range(k + 1, STRIP):
                cols[b] = jnp.where(at, 0.0, cols[b]) - both * spread(cols[b], k)
            row_a, row_e = spread(full_a, k), spread(full_e, k)
            down_a = down_a - below * spread(down_a, k)
            down_e = down_e - below * spread(down_e, k)
            full_a = jnp.where(at, 0.0, full_a) - both * row_a
            full_e = jnp.where(at, 0.0, full_e) - both * row_e
            pivots = pivot if pivots is None else jnp.where(sub >= k, pivot, pivots)
        scale = lax.rsqrt(pivots)
        u_ref[base + first:base + first + STRIP, base:base + n] = jnp.where(lane >= sub + first, down_a * scale, 0.0)
        inverse_ref[here, :] = down_e * scale
        spread_a = [spread(full_a, k) for k in range(STRIP)]
        spread_e = [spread(full_e, k) for k in range(STRIP)]
        for i in range(s + 1, strips):
            next_a, next_e = rows_a[i], rows_e[i]
            for k in range(STRIP):
                c = jnp.broadcast_to(rows_a[i][:, first + k:first + k + 1], (STRIP, n))
                next_a = next_a - c * spread_a[k]
                next_e = next_e - c * spread_e[k]
            rows_a[i], rows_e[i] = next_a, next_e


def factor_and_solve(gram_ref, applied_ref, states_ref, u_ref, work, inverse):
    n = gram_ref.shape[1]
    size = u_ref.shape[0]
    nblocks = size // n
    at = 0
    for j in range(nblocks):
        for k in range(j, nblocks):
            work[n * j:n * (j + 1), n * k:n * (k + 1)] = gram_ref[at]
            at += 1
    states_ref[...] = applied_ref[...]
    u_ref[...] = jnp.zeros_like(u_ref)
    for j in range(nblocks):
        lo, hi = n * j, n * (j + 1)
        factor_diagonal(work.at[lo:hi, lo:hi], inverse, u_ref, lo, n)
        inv = inverse[...]
        solved = dot_full(states_ref[:, lo:hi], inv, 1, 1)
        states_ref[:, lo:hi] = solved
        if hi < size:
            panel = dot_full(inv, work[lo:hi, hi:], 1, 0)
            u_ref[lo:hi, hi:] = panel
            for k in range(j + 1, nblocks):
                a, b = n * k, n * (k + 1)
                work[a:b, a:] -= dot_full(panel[:, a - hi:b - hi], panel[:, a - hi:], 0, 0)
            states_ref[:, hi:] -= dot_full(solved, panel, 1, 0)


def call(body, outs, in_spaces, scratch=(), out_space=pltpu.VMEM, mib=40):
    return pl.pallas_call(
        body,
        out_shape=outs,
        in_specs=[pl.BlockSpec(memory_space=space) for space in in_spaces],
        out_specs=[pl.BlockSpec(memory_space=out_space) for _ in outs],
        scratch_shapes=list(scratch),
        compiler_params=pltpu.CompilerParams(vmem_limit_bytes=mib * 2**20),
    )


def move(value, by_core):
    ny, nz, nk = (lax.axis_size(axis) for axis in ("y", "z", "k"))
    pairs = []
    for y in range(ny):
        for z in range(nz):
            for k in range(nk):
                to_y, to_z = by_core[k](y, z)
                pairs.append(((y * nz + z) * nk + k, ((to_y % ny) * nz + to_z % nz) * nk + k))
    return lax.ppermute(value, ("y", "z", "k"), pairs)


def gather_states(vectors):
    held = vectors[None]
    for bit in (4, 2, 1):
        other = move(held, [lambda y, z: (y, z ^ bit), lambda y, z: (y ^ bit, z)])
        held = jnp.concatenate([held, other])
    up = [lambda y, z: (y + 1, z), lambda y, z: (y, z + 1)]
    down = [lambda y, z: (y - 1, z), lambda y, z: (y, z - 1)]
    half = held.shape[0] // 2
    above, below = [held], [held]
    for _ in range(3):
        above.append(move(above[-1], up))
        below.append(move(below[-1], down))
    last_above = move(above[-1][:half], up)
    last_below = move(below[-1][half:], down)
    return above + [last_above] + below[:0:-1] + [last_below]


def where_blocks(cols, y, z, k):
    from_y, from_z = cols // 8, cols % 8
    near = jnp.where(k == 0, from_z ^ z, from_y ^ y)
    far = jnp.where(k == 0, y - from_y, z - from_z) % 8
    place = near // 4 + near // 2 % 2 * 2 + near % 2 * 4
    source = jnp.where((far == 4) & (place >= 4), 8, far)
    return source, jnp.where(far == 4, place % 4, place)


def per_device(vectors, onsite, tile_values, tile_rows, tile_cols, tile_count):
    own_rows, kstates = vectors.shape
    width = tile_values.shape[-1]
    slots = tile_values.shape[2]
    f32 = jnp.float32
    vm, sm, anywhere = pltpu.VMEM, pltpu.SMEM, pl.ANY
    halves = lax.axis_size("x")
    y, z, k = (lax.axis_index(axis) for axis in ("y", "z", "k"))

    rows = tile_rows.reshape(slots)
    source, place = where_blocks(tile_cols.reshape(slots), y, z, k)
    meta = jnp.concatenate([(rows + k) % 2 * halves + rows // 2, source, place, tile_count.reshape(1)])
    local = onsite[:, None] * vectors.astype(f32)
    buffers = gather_states(vectors)

    part = jax.ShapeDtypeStruct((halves, width, kstates), f32)
    keep, send = call(
        tile_products,
        [part, part],
        [sm, anywhere] + [anywhere] * len(buffers),
        [
            vm((2 * halves, width, kstates), f32),
            vm((slots, width, width), jnp.bfloat16),
            vm((slots, width, kstates), jnp.bfloat16),
            pltpu.SemaphoreType.DMA,
            pltpu.SemaphoreType.DMA((slots,)),
            pltpu.SemaphoreType.DMA((2,)),
        ],
        anywhere,
        20,
    )(meta, tile_values[0, 0], *buffers)
    other = lax.ppermute(send, "k", [(0, 1), (1, 0)])
    parts = lax.all_to_all(keep + other, "x", 0, 0, tiled=True)

    nblocks = kstates // width
    upper_blocks = nblocks * (nblocks + 1) // 2
    applied, gram = call(
        gram_blocks,
        [jax.ShapeDtypeStruct((own_rows, kstates), f32), jax.ShapeDtypeStruct((upper_blocks, width, width), f32)],
        [vm, vm],
    )(parts, local)

    ncol = lax.axis_size(("x", "k"))
    nrow = lax.axis_size(("y", "z"))
    piece = lax.all_to_all(gram.reshape(ncol, -1, width), ("x", "k"), 0, 0, tiled=True).sum(0)
    shape = piece.shape
    piece = lax.all_to_all(piece.reshape(nrow, -1), ("y", "z"), 0, 0, tiled=True).sum(0, keepdims=True)
    piece = lax.all_to_all(jnp.tile(piece, (nrow, 1)), ("y", "z"), 0, 0, tiled=True).reshape(shape)
    gram = lax.all_to_all(jnp.tile(piece[None], (ncol, 1, 1)), ("x", "k"), 0, 0, tiled=True)
    gram = gram.reshape(upper_blocks, width, width)

    states, upper = call(
        factor_and_solve,
        [jax.ShapeDtypeStruct((own_rows, kstates), f32), jax.ShapeDtypeStruct((kstates, kstates), f32)],
        [vm, vm],
        [vm((kstates, kstates), f32), vm((width, width), f32)],
    )(gram, applied)
    return (states, upper)


def solution(mesh):
    fine = Mesh(mesh.devices.reshape(8, 8, 4, 2), ("y", "z", "x", "k"))
    row, col = ("y", "z"), ("x", "k")
    return jax.shard_map(
        per_device,
        mesh=fine,
        in_specs=(
            P(row + col, None),
            P(row + col),
            P(row, col, None, None, None),
            P(row, col, None),
            P(row, col, None),
            P(row, col),
        ),
        out_specs=(P(row + col, None), P()),
        check_vma=False,
    )
```

```python
import functools

import jax
import jax.numpy as jnp
from jax import lax
from jax.experimental import pallas as pl
from jax.experimental.pallas import tpu as pltpu
from jax.sharding import Mesh, PartitionSpec as P

FULL = lax.Precision.HIGHEST
STRIP = 8
GROUP = 3


def dot_full(left, right, left_dim, right_dim):
    dims = (((left_dim,), (right_dim,)), ((), ()))
    return lax.dot_general(left, right, dims, precision=FULL, preferred_element_type=jnp.float32)


def tile_products(meta_ref, tiles_ref, *refs):
    *sources, keep_ref, send_ref, sums, tiles, held, tile_sem, sems, out_sems = refs
    slots = tiles_ref.shape[0]
    per_core = keep_ref.shape[0]
    count = meta_ref[3 * slots]
    steps = (count + GROUP - 1) // GROUP

    fetch_tiles = pltpu.make_async_copy(tiles_ref, tiles, tile_sem)
    fetch_tiles.start()

    @pl.loop(0, steps * GROUP)
    def _(t):
        for at, source in enumerate(sources):
            @pl.when(meta_ref[slots + t] == at)
            def _():
                pltpu.make_async_copy(source.at[meta_ref[2 * slots + t]], held.at[t], sems.at[t]).start()

    sums[...] = jnp.zeros_like(sums)
    fetch_tiles.wait()

    @pl.loop(0, steps)
    def _(step):
        first = step * GROUP
        prods = []
        for t in range(GROUP):
            pltpu.make_async_copy(sources[0].at[0], held.at[first + t], sems.at[first + t]).wait()
            tile = tiles[first + t]
            tile = jnp.where(first + t < count, tile, jnp.zeros_like(tile))
            prods.append(jnp.dot(tile, held[first + t], preferred_element_type=jnp.float32))
        for t in range(GROUP):
            sums[meta_ref[first + t]] += prods[t]

    put_keep = pltpu.make_async_copy(sums.at[:per_core], keep_ref, out_sems.at[0])
    put_send = pltpu.make_async_copy(sums.at[per_core:], send_ref, out_sems.at[1])
    put_send.start()
    put_keep.start()
    put_send.wait()
    put_keep.wait()


def gram_blocks(parts_ref, local_ref, applied_ref, gram_ref):
    width = gram_ref.shape[1]
    applied = local_ref[...]
    for i in range(parts_ref.shape[0]):
        applied = applied + parts_ref[i]
    applied_ref[...] = applied
    nblocks = applied.shape[1] // width
    at = 0
    for j in range(nblocks):
        row = dot_full(applied[:, j * width:(j + 1) * width], applied[:, j * width:], 0, 0)
        for k in range(nblocks - j):
            gram_ref[at] = row[:, k * width:(k + 1) * width]
            at += 1


def factor_diagonal(a_ref, inverse_ref, u_ref, base, n):
    sub = lax.broadcasted_iota(jnp.int32, (STRIP, n), 0)
    lane = lax.broadcasted_iota(jnp.int32, (STRIP, n), 1)
    strips = n // STRIP

    def spread(rows, k):
        return jnp.broadcast_to(rows[k:k + 1, :], (STRIP, n))

    rows_a = [a_ref[STRIP * i:STRIP * (i + 1), :] for i in range(strips)]
    rows_e = [jnp.where(lane == sub + STRIP * i, 1.0, 0.0) for i in range(strips)]
    for s in range(strips):
        first = STRIP * s
        here = slice(first, first + STRIP)
        cols = [jnp.broadcast_to(rows_a[s][:, first + k:first + k + 1], (STRIP, n)) for k in range(STRIP)]
        down_a, down_e = rows_a[s], rows_e[s]
        full_a, full_e = rows_a[s], rows_e[s]
        pivots = None
        for k in range(STRIP):
            pivot = spread(cols[k], k)
            recip = 1.0 / pivot
            ratio = cols[k] * recip
            at = sub == k
            both = jnp.where(at, -recip, ratio)
            below = jnp.where(sub > k, ratio, 0.0)
            for b in range(k + 1, STRIP):
                cols[b] = jnp.where(at, 0.0, cols[b]) - both * spread(cols[b], k)
            row_a, row_e = spread(full_a, k), spread(full_e, k)
            down_a = down_a - below * spread(down_a, k)
            down_e = down_e - below * spread(down_e, k)
            full_a = jnp.where(at, 0.0, full_a) - both * row_a
            full_e = jnp.where(at, 0.0, full_e) - both * row_e
            pivots = pivot if pivots is None else jnp.where(sub >= k, pivot, pivots)
        scale = lax.rsqrt(pivots)
        u_ref[base + first:base + first + STRIP, base:base + n] = jnp.where(lane >= sub + first, down_a * scale, 0.0)
        inverse_ref[here, :] = down_e * scale
        spread_a = [spread(full_a, k) for k in range(STRIP)]
        spread_e = [spread(full_e, k) for k in range(STRIP)]
        for i in range(s + 1, strips):
            next_a, next_e = rows_a[i], rows_e[i]
            for k in range(STRIP):
                c = jnp.broadcast_to(rows_a[i][:, first + k:first + k + 1], (STRIP, n))
                next_a = next_a - c * spread_a[k]
                next_e = next_e - c * spread_e[k]
            rows_a[i], rows_e[i] = next_a, next_e


def factor_and_solve(gram_ref, applied_ref, states_ref, u_ref, work, inverse):
    n = gram_ref.shape[1]
    size = u_ref.shape[0]
    nblocks = size // n
    at = 0
    for j in range(nblocks):
        for k in range(j, nblocks):
            work[n * j:n * (j + 1), n * k:n * (k + 1)] = gram_ref[at]
            at += 1
    states_ref[...] = applied_ref[...]
    u_ref[...] = jnp.zeros_like(u_ref)
    for j in range(nblocks):
        lo, hi = n * j, n * (j + 1)
        factor_diagonal(work.at[lo:hi, lo:hi], inverse, u_ref, lo, n)
        inv = inverse[...]
        solved = dot_full(states_ref[:, lo:hi], inv, 1, 1)
        states_ref[:, lo:hi] = solved
        if hi < size:
            panel = dot_full(inv, work[lo:hi, hi:], 1, 0)
            u_ref[lo:hi, hi:] = panel
            for k in range(j + 1, nblocks):
                a, b = n * k, n * (k + 1)
                work[a:b, a:] -= dot_full(panel[:, a - hi:b - hi], panel[:, a - hi:], 0, 0)
            states_ref[:, hi:] -= dot_full(solved, panel, 1, 0)


def call(body, outs, in_spaces, scratch=(), out_space=pltpu.VMEM, mib=40):
    return pl.pallas_call(
        body,
        out_shape=outs,
        in_specs=[pl.BlockSpec(memory_space=space) for space in in_spaces],
        out_specs=[pl.BlockSpec(memory_space=out_space) for _ in outs],
        scratch_shapes=list(scratch),
        compiler_params=pltpu.CompilerParams(vmem_limit_bytes=mib * 2**20),
    )


def line_places(ny, nz, nk):
    lines = []
    for fixed in range(ny):
        for k in range(nk):
            line = []
            for along in range(nz):
                y, z = (fixed, along) if k == 0 else (along, fixed)
                line.append((y * nz + z) * nk + k)
            lines.append(line)
    return lines


def ring_pairs(ny, nz, nk, step):
    pairs = []
    for y in range(ny):
        for z in range(nz):
            for k in range(nk):
                to_y, to_z = ((y + step) % ny, z) if k == 0 else (y, (z + step) % nz)
                pairs.append(((y * nz + z) * nk + k, (to_y * nz + to_z) * nk + k))
    return pairs


def gather_states(vectors):
    axes = ("y", "z", "k")
    sizes = tuple(lax.axis_size(axis) for axis in axes)
    copies = jnp.broadcast_to(vectors[None], (sizes[1],) + vectors.shape)
    line = lax.all_to_all(copies, axes, 0, 0, axis_index_groups=line_places(*sizes), tiled=True)
    half = line.shape[0] // 2
    up, down = ring_pairs(*sizes, 1), ring_pairs(*sizes, -1)
    halves = [line[:half], line[half:]]
    above, below = [[h] for h in halves], [[h] for h in halves]
    for step in range(4):
        for at in (0, 1):
            if step < 3 or at == 0:
                above[at].append(lax.ppermute(above[at][-1], axes, up))
            if step < 3 or at == 1:
                below[at].append(lax.ppermute(below[at][-1], axes, down))
    return above[0] + below[0][:0:-1] + above[1] + below[1][:0:-1]


def where_blocks(cols, y, z, k):
    from_y, from_z = cols // 8, cols % 8
    near = jnp.where(k == 0, from_z, from_y)
    far = jnp.where(k == 0, y - from_y, z - from_z) % 8
    return near // 4 * 8 + far, near % 4


def per_device(vectors, onsite, tile_values, tile_rows, tile_cols, tile_count):
    own_rows, kstates = vectors.shape
    width = tile_values.shape[-1]
    slots = tile_values.shape[2]
    f32 = jnp.float32
    vm, sm, anywhere = pltpu.VMEM, pltpu.SMEM, pl.ANY
    halves = lax.axis_size("x")
    y, z, k = (lax.axis_index(axis) for axis in ("y", "z", "k"))

    rows = tile_rows.reshape(slots)
    source, place = where_blocks(tile_cols.reshape(slots), y, z, k)
    meta = jnp.concatenate([(rows + k) % 2 * halves + rows // 2, source, place, tile_count.reshape(1)])
    local = onsite[:, None] * vectors.astype(f32)
    buffers = gather_states(vectors)

    part = jax.ShapeDtypeStruct((halves, width, kstates), f32)
    keep, send = call(
        tile_products,
        [part, part],
        [sm, anywhere] + [anywhere] * len(buffers),
        [
            vm((2 * halves, width, kstates), f32),
            vm((slots, width, width), jnp.bfloat16),
            vm((slots, width, kstates), jnp.bfloat16),
            pltpu.SemaphoreType.DMA,
            pltpu.SemaphoreType.DMA((slots,)),
            pltpu.SemaphoreType.DMA((2,)),
        ],
        anywhere,
        57,
    )(meta, tile_values[0, 0], *buffers)
    other = lax.ppermute(send, "k", [(0, 1), (1, 0)])
    parts = lax.all_to_all(keep + other, "x", 0, 0, tiled=True)

    nblocks = kstates // width
    upper_blocks = nblocks * (nblocks + 1) // 2
    applied, gram = call(
        gram_blocks,
        [jax.ShapeDtypeStruct((own_rows, kstates), f32), jax.ShapeDtypeStruct((upper_blocks, width, width), f32)],
        [vm, vm],
    )(parts, local)

    ncol = lax.axis_size(("x", "k"))
    nrow = lax.axis_size(("y", "z"))
    piece = lax.all_to_all(gram.reshape(ncol, -1, width), ("x", "k"), 0, 0, tiled=True).sum(0)
    shape = piece.shape
    piece = lax.all_to_all(piece.reshape(nrow, -1), ("y", "z"), 0, 0, tiled=True).sum(0, keepdims=True)
    piece = lax.all_to_all(jnp.tile(piece, (nrow, 1)), ("y", "z"), 0, 0, tiled=True).reshape(shape)
    gram = lax.all_to_all(jnp.tile(piece[None], (ncol, 1, 1)), ("x", "k"), 0, 0, tiled=True)
    gram = gram.reshape(upper_blocks, width, width)

    states, upper = call(
        factor_and_solve,
        [jax.ShapeDtypeStruct((own_rows, kstates), f32), jax.ShapeDtypeStruct((kstates, kstates), f32)],
        [vm, vm],
        [vm((kstates, kstates), f32), vm((width, width), f32)],
    )(gram, applied)
    return (states, upper)


def solution(mesh):
    fine = Mesh(mesh.devices.reshape(8, 8, 4, 2), ("y", "z", "x", "k"))
    row, col = ("y", "z"), ("x", "k")
    return jax.shard_map(
        per_device,
        mesh=fine,
        in_specs=(
            P(row + col, None),
            P(row + col),
            P(row, col, None, None, None),
            P(row, col, None),
            P(row, col, None),
            P(row, col),
        ),
        out_specs=(P(row + col, None), P()),
        check_vma=False,
    )
```

```python
import functools

import jax
import jax.numpy as jnp
from jax import lax
from jax.experimental import pallas as pl
from jax.experimental.pallas import tpu as pltpu
from jax.sharding import Mesh, PartitionSpec as P

FULL = lax.Precision.HIGHEST
STRIP = 8
GROUP = 3


def dot_full(left, right, left_dim, right_dim):
    dims = (((left_dim,), (right_dim,)), ((), ()))
    return lax.dot_general(left, right, dims, precision=FULL, preferred_element_type=jnp.float32)


def tile_products(meta_ref, tiles_ref, *refs):
    *sources, keep_ref, send_ref, sums, tiles, held, tile_sem, sems, out_sems = refs
    slots = tiles_ref.shape[0]
    per_core = keep_ref.shape[0]
    count = meta_ref[3 * slots]
    steps = (count + GROUP - 1) // GROUP

    fetch_tiles = pltpu.make_async_copy(tiles_ref, tiles, tile_sem)
    fetch_tiles.start()

    @pl.loop(0, steps * GROUP)
    def _(t):
        for at, source in enumerate(sources):
            @pl.when(meta_ref[slots + t] == at)
            def _():
                pltpu.make_async_copy(source.at[meta_ref[2 * slots + t]], held.at[t], sems.at[t]).start()

    sums[...] = jnp.zeros_like(sums)
    fetch_tiles.wait()

    @pl.loop(0, steps)
    def _(step):
        first = step * GROUP
        prods = []
        for t in range(GROUP):
            pltpu.make_async_copy(sources[0].at[0], held.at[first + t], sems.at[first + t]).wait()
            tile = tiles[first + t]
            tile = jnp.where(first + t < count, tile, jnp.zeros_like(tile))
            prods.append(jnp.dot(tile, held[first + t], preferred_element_type=jnp.float32))
        for t in range(GROUP):
            sums[meta_ref[first + t]] += prods[t]

    put_keep = pltpu.make_async_copy(sums.at[:per_core], keep_ref, out_sems.at[0])
    put_send = pltpu.make_async_copy(sums.at[per_core:], send_ref, out_sems.at[1])
    put_send.start()
    put_keep.start()
    put_send.wait()
    put_keep.wait()


def upper_pairs(nblocks):
    pairs = [(j, k) for j in range(nblocks) for k in range(j, nblocks)]
    return pairs[:len(pairs) // 2], pairs[len(pairs) // 2:]


def gram_blocks(core_ref, parts_ref, local_ref, applied_ref, own_ref, other_ref):
    n = own_ref.shape[1]
    applied = local_ref[...]
    for i in range(parts_ref.shape[0]):
        applied = applied + parts_ref[i]
    applied_ref[...] = applied
    nblocks = applied.shape[1] // n
    rows = [dot_full(applied[:, j * n:(j + 1) * n], applied[:, j * n:], 0, 0) for j in range(nblocks)]
    for core in (0, 1):
        @pl.when(core_ref[0] == core)
        def _():
            for half, pairs in enumerate(upper_pairs(nblocks)):
                target = own_ref if half == core else other_ref
                for at, (j, k) in enumerate(pairs):
                    target[at] = rows[j][:, (k - j) * n:(k - j + 1) * n]


def factor_diagonal(a_ref, inverse_ref, u_ref, base, n):
    sub = lax.broadcasted_iota(jnp.int32, (STRIP, n), 0)
    lane = lax.broadcasted_iota(jnp.int32, (STRIP, n), 1)
    strips = n // STRIP

    def spread(rows, k):
        return jnp.broadcast_to(rows[k:k + 1, :], (STRIP, n))

    rows_a = [a_ref[STRIP * i:STRIP * (i + 1), :] for i in range(strips)]
    rows_e = [jnp.where(lane == sub + STRIP * i, 1.0, 0.0) for i in range(strips)]
    for s in range(strips):
        first = STRIP * s
        here = slice(first, first + STRIP)
        cols = [jnp.broadcast_to(rows_a[s][:, first + k:first + k + 1], (STRIP, n)) for k in range(STRIP)]
        down_a, down_e = rows_a[s], rows_e[s]
        full_a, full_e = rows_a[s], rows_e[s]
        pivots = None
        for k in range(STRIP):
            pivot = spread(cols[k], k)
            recip = 1.0 / pivot
            ratio = cols[k] * recip
            at = sub == k
            both = jnp.where(at, -recip, ratio)
            below = jnp.where(sub > k, ratio, 0.0)
            for b in range(k + 1, STRIP):
                cols[b] = jnp.where(at, 0.0, cols[b]) - both * spread(cols[b], k)
            row_a, row_e = spread(full_a, k), spread(full_e, k)
            down_a = down_a - below * spread(down_a, k)
            down_e = down_e - below * spread(down_e, k)
            full_a = jnp.where(at, 0.0, full_a) - both * row_a
            full_e = jnp.where(at, 0.0, full_e) - both * row_e
            pivots = pivot if pivots is None else jnp.where(sub >= k, pivot, pivots)
        scale = lax.rsqrt(pivots)
        u_ref[base + first:base + first + STRIP, base:base + n] = jnp.where(lane >= sub + first, down_a * scale, 0.0)
        inverse_ref[here, :] = down_e * scale
        spread_a = [spread(full_a, k) for k in range(STRIP)]
        spread_e = [spread(full_e, k) for k in range(STRIP)]
        for i in range(s + 1, strips):
            next_a, next_e = rows_a[i], rows_e[i]
            for k in range(STRIP):
                c = jnp.broadcast_to(rows_a[i][:, first + k:first + k + 1], (STRIP, n))
                next_a = next_a - c * spread_a[k]
                next_e = next_e - c * spread_e[k]
            rows_a[i], rows_e[i] = next_a, next_e


def factor_and_solve(core_ref, own_ref, other_ref, applied_ref, states_ref, u_ref, work, inverse):
    n = own_ref.shape[1]
    size = u_ref.shape[0]
    nblocks = size // n
    for core in (0, 1):
        @pl.when(core_ref[0] == core)
        def _():
            for half, pairs in enumerate(upper_pairs(nblocks)):
                source = own_ref if half == core else other_ref
                for at, (j, k) in enumerate(pairs):
                    work[n * j:n * (j + 1), n * k:n * (k + 1)] = source[at]
    states_ref[...] = applied_ref[...]
    u_ref[...] = jnp.zeros_like(u_ref)
    for j in range(nblocks):
        lo, hi = n * j, n * (j + 1)
        factor_diagonal(work.at[lo:hi, lo:hi], inverse, u_ref, lo, n)
        inv = inverse[...]
        solved = dot_full(states_ref[:, lo:hi], inv, 1, 1)
        states_ref[:, lo:hi] = solved
        if hi < size:
            panel = dot_full(inv, work[lo:hi, hi:], 1, 0)
            u_ref[lo:hi, hi:] = panel
            for k in range(j + 1, nblocks):
                a, b = n * k, n * (k + 1)
                work[a:b, a:] -= dot_full(panel[:, a - hi:b - hi], panel[:, a - hi:], 0, 0)
            states_ref[:, hi:] -= dot_full(solved, panel, 1, 0)


def call(body, outs, in_spaces, scratch=(), out_space=pltpu.VMEM, mib=40):
    return pl.pallas_call(
        body,
        out_shape=outs,
        in_specs=[pl.BlockSpec(memory_space=space) for space in in_spaces],
        out_specs=[pl.BlockSpec(memory_space=out_space) for _ in outs],
        scratch_shapes=list(scratch),
        compiler_params=pltpu.CompilerParams(vmem_limit_bytes=mib * 2**20),
    )


def line_places(ny, nz, nk):
    lines = []
    for fixed in range(ny):
        for k in range(nk):
            line = []
            for along in range(nz):
                y, z = (fixed, along) if k == 0 else (along, fixed)
                line.append((y * nz + z) * nk + k)
            lines.append(line)
    return lines


def ring_pairs(ny, nz, nk, step):
    pairs = []
    for y in range(ny):
        for z in range(nz):
            for k in range(nk):
                to_y, to_z = ((y + step) % ny, z) if k == 0 else (y, (z + step) % nz)
                pairs.append(((y * nz + z) * nk + k, (to_y * nz + to_z) * nk + k))
    return pairs


def gather_states(vectors):
    axes = ("y", "z", "k")
    sizes = tuple(lax.axis_size(axis) for axis in axes)
    copies = jnp.broadcast_to(vectors[None], (sizes[1],) + vectors.shape)
    line = lax.all_to_all(copies, axes, 0, 0, axis_index_groups=line_places(*sizes), tiled=True)
    half = line.shape[0] // 2
    up, down = ring_pairs(*sizes, 1), ring_pairs(*sizes, -1)
    halves = [line[:half], line[half:]]
    above, below = [[h] for h in halves], [[h] for h in halves]
    for step in range(4):
        for at in (0, 1):
            if step < 3 or at == 0:
                above[at].append(lax.ppermute(above[at][-1], axes, up))
            if step < 3 or at == 1:
                below[at].append(lax.ppermute(below[at][-1], axes, down))
    return above[0] + below[0][:0:-1] + above[1] + below[1][:0:-1]


def where_blocks(cols, y, z, k):
    from_y, from_z = cols // 8, cols % 8
    near = jnp.where(k == 0, from_z, from_y)
    far = jnp.where(k == 0, y - from_y, z - from_z) % 8
    return near // 4 * 8 + far, near % 4


def sum_groups(ny, nz, nx, nk):
    def device(y, z, x, k):
        return ((y * nz + z) * nx + x) * nk + k

    four, same = [], []
    for y in range(ny):
        for z in range(nz):
            four.append([device(y, z, x, 0) for x in range(nx)])
    for x in range(nx):
        same.append([device(y, z, x, 0) for y in range(ny) for z in range(nz)])
        for y in range(0, ny, 2):
            for z in range(0, nz, 2):
                four.append([device(y + i, z + j, x, 1) for i in (0, 1) for j in (0, 1)])
    for i in (0, 1):
        for j in (0, 1):
            same.append([
                device(y + i, z + j, x, 1)
                for x in range(nx) for y in range(0, ny, 2) for z in range(0, nz, 2)
            ])
    return four, same


def sum_halves(value):
    axes = ("y", "z", "x", "k")
    four, same = sum_groups(*(lax.axis_size(axis) for axis in axes))

    def exchange(pieces, groups):
        return lax.all_to_all(pieces, axes, 0, 0, axis_index_groups=groups, tiled=True)

    def copies(piece, groups):
        return jnp.broadcast_to(piece[None], (len(groups[0]),) + piece.shape)

    part = exchange(value.reshape(len(four[0]), -1, value.shape[-1]), four).sum(0)
    piece = exchange(part.reshape(len(same[0]), -1), same).sum(0)
    part = exchange(copies(piece, same), same).reshape(part.shape)
    return exchange(copies(part, four), four).reshape(value.shape)


def per_device(vectors, onsite, tile_values, tile_rows, tile_cols, tile_count):
    own_rows, kstates = vectors.shape
    width = tile_values.shape[-1]
    slots = tile_values.shape[2]
    f32 = jnp.float32
    vm, sm, anywhere = pltpu.VMEM, pltpu.SMEM, pl.ANY
    halves = lax.axis_size("x")
    y, z, k = (lax.axis_index(axis) for axis in ("y", "z", "k"))

    rows = tile_rows.reshape(slots)
    source, place = where_blocks(tile_cols.reshape(slots), y, z, k)
    meta = jnp.concatenate([(rows + k) % 2 * halves + rows // 2, source, place, tile_count.reshape(1)])
    local = onsite[:, None] * vectors.astype(f32)
    buffers = gather_states(vectors)

    part = jax.ShapeDtypeStruct((halves, width, kstates), f32)
    keep, send = call(
        tile_products,
        [part, part],
        [sm, anywhere] + [anywhere] * len(buffers),
        [
            vm((2 * halves, width, kstates), f32),
            vm((slots, width, width), jnp.bfloat16),
            vm((slots, width, kstates), jnp.bfloat16),
            pltpu.SemaphoreType.DMA,
            pltpu.SemaphoreType.DMA((slots,)),
            pltpu.SemaphoreType.DMA((2,)),
        ],
        anywhere,
        57,
    )(meta, tile_values[0, 0], *buffers)
    other = lax.ppermute(send, "k", [(0, 1), (1, 0)])
    parts = lax.all_to_all(keep + other, "x", 0, 0, tiled=True)

    nblocks = kstates // width
    half = jax.ShapeDtypeStruct((nblocks * (nblocks + 1) // 4, width, width), f32)
    core = k.astype(jnp.int32).reshape(1)
    applied, own, other = call(
        gram_blocks,
        [jax.ShapeDtypeStruct((own_rows, kstates), f32), half, half],
        [sm, vm, vm],
    )(core, parts, local)
    own = sum_halves(own + lax.ppermute(other, "k", [(0, 1), (1, 0)]))
    other = lax.ppermute(own, "k", [(0, 1), (1, 0)])

    states, upper = call(
        factor_and_solve,
        [jax.ShapeDtypeStruct((own_rows, kstates), f32), jax.ShapeDtypeStruct((kstates, kstates), f32)],
        [sm, vm, vm, vm],
        [vm((kstates, kstates), f32), vm((width, width), f32)],
    )(core, own, other, applied)
    return (states, upper)


def solution(mesh):
    fine = Mesh(mesh.devices.reshape(8, 8, 4, 2), ("y", "z", "x", "k"))
    row, col = ("y", "z"), ("x", "k")
    return jax.shard_map(
        per_device,
        mesh=fine,
        in_specs=(
            P(row + col, None),
            P(row + col),
            P(row, col, None, None, None),
            P(row, col, None),
            P(row, col, None),
            P(row, col),
        ),
        out_specs=(P(row + col, None), P()),
        check_vma=False,
    )
```

```python
import functools

import jax
import jax.numpy as jnp
from jax import lax
from jax.experimental import pallas as pl
from jax.experimental.pallas import tpu as pltpu
from jax.sharding import Mesh, PartitionSpec as P

FULL = lax.Precision.HIGHEST
STRIP = 8


def dot_full(left, right, left_dim, right_dim):
    dims = (((left_dim,), (right_dim,)), ((), ()))
    return lax.dot_general(left, right, dims, precision=FULL, preferred_element_type=jnp.float32)


def tile_products(meta_ref, tiles_ref, *refs):
    *sources, keep_ref, send_ref, sums = refs
    slots = tiles_ref.shape[0]
    per_core = keep_ref.shape[0]
    sums[...] = jnp.zeros_like(sums)

    def add(t, which, first, last):
        if last - first == 1:
            block = sources[first][meta_ref[2 * slots + t]]
            sums[meta_ref[t]] += jnp.dot(tiles_ref[t], block, preferred_element_type=jnp.float32)
            return
        middle = (first + last) // 2
        pl.when(which < middle)(lambda: add(t, which, first, middle))
        pl.when(which >= middle)(lambda: add(t, which, middle, last))

    @pl.loop(0, meta_ref[3 * slots])
    def _(t):
        add(t, meta_ref[slots + t], 0, len(sources))

    keep_ref[...] = sums[:per_core]
    send_ref[...] = sums[per_core:]


def upper_pairs(nblocks):
    pairs = [(j, k) for j in range(nblocks) for k in range(j, nblocks)]
    return pairs[:len(pairs) // 2], pairs[len(pairs) // 2:]


def gram_blocks(core_ref, parts_ref, local_ref, applied_ref, own_ref, other_ref):
    n = own_ref.shape[1]
    applied = local_ref[...]
    for i in range(parts_ref.shape[0]):
        applied = applied + parts_ref[i]
    applied_ref[...] = applied
    nblocks = applied.shape[1] // n
    rows = [dot_full(applied[:, j * n:(j + 1) * n], applied[:, j * n:], 0, 0) for j in range(nblocks)]
    for core in (0, 1):
        @pl.when(core_ref[0] == core)
        def _():
            for half, pairs in enumerate(upper_pairs(nblocks)):
                target = own_ref if half == core else other_ref
                for at, (j, k) in enumerate(pairs):
                    target[at] = rows[j][:, (k - j) * n:(k - j + 1) * n]


def factor_diagonal(a_ref, inverse_ref, u_ref, base, n):
    sub = lax.broadcasted_iota(jnp.int32, (STRIP, n), 0)
    lane = lax.broadcasted_iota(jnp.int32, (STRIP, n), 1)
    strips = n // STRIP

    def spread(rows, k):
        return jnp.broadcast_to(rows[k:k + 1, :], (STRIP, n))

    rows_a = [a_ref[STRIP * i:STRIP * (i + 1), :] for i in range(strips)]
    rows_e = [jnp.where(lane == sub + STRIP * i, 1.0, 0.0) for i in range(strips)]
    for s in range(strips):
        first = STRIP * s
        here = slice(first, first + STRIP)
        cols = [jnp.broadcast_to(rows_a[s][:, first + k:first + k + 1], (STRIP, n)) for k in range(STRIP)]
        down_a, down_e = rows_a[s], rows_e[s]
        full_a, full_e = rows_a[s], rows_e[s]
        pivots = None
        for k in range(STRIP):
            pivot = spread(cols[k], k)
            recip = 1.0 / pivot
            at = sub == k
            both = jnp.where(at, -1.0, cols[k])
            below = jnp.where(sub > k, cols[k], 0.0)
            for b in range(k + 1, STRIP):
                cols[b] = jnp.where(at, 0.0, cols[b]) - (both * spread(cols[b], k)) * recip
            row_a, row_e = spread(full_a, k), spread(full_e, k)
            down_a = down_a - (below * spread(down_a, k)) * recip
            down_e = down_e - (below * spread(down_e, k)) * recip
            full_a = jnp.where(at, 0.0, full_a) - (both * row_a) * recip
            full_e = jnp.where(at, 0.0, full_e) - (both * row_e) * recip
            pivots = pivot if pivots is None else jnp.where(sub >= k, pivot, pivots)
        scale = lax.rsqrt(pivots)
        u_ref[base + first:base + first + STRIP, base:base + n] = jnp.where(lane >= sub + first, down_a * scale, 0.0)
        inverse_ref[here, :] = down_e * scale
        spread_a = [spread(full_a, k) for k in range(STRIP)]
        spread_e = [spread(full_e, k) for k in range(STRIP)]
        for i in range(s + 1, strips):
            next_a, next_e = rows_a[i], rows_e[i]
            for k in range(STRIP):
                c = jnp.broadcast_to(rows_a[i][:, first + k:first + k + 1], (STRIP, n))
                next_a = next_a - c * spread_a[k]
                next_e = next_e - c * spread_e[k]
            rows_a[i], rows_e[i] = next_a, next_e


def factor_and_solve(core_ref, own_ref, other_ref, applied_ref, states_ref, u_ref, work, inverse):
    n = own_ref.shape[1]
    size = u_ref.shape[0]
    nblocks = size // n
    for core in (0, 1):
        @pl.when(core_ref[0] == core)
        def _():
            for half, pairs in enumerate(upper_pairs(nblocks)):
                source = own_ref if half == core else other_ref
                for at, (j, k) in enumerate(pairs):
                    work[n * j:n * (j + 1), n * k:n * (k + 1)] = source[at]
    states_ref[...] = applied_ref[...]
    u_ref[...] = jnp.zeros_like(u_ref)
    for j in range(nblocks):
        lo, hi = n * j, n * (j + 1)
        factor_diagonal(work.at[lo:hi, lo:hi], inverse, u_ref, lo, n)
        inv = inverse[...]
        solved = dot_full(states_ref[:, lo:hi], inv, 1, 1)
        states_ref[:, lo:hi] = solved
        if hi < size:
            panel = dot_full(inv, work[lo:hi, hi:], 1, 0)
            u_ref[lo:hi, hi:] = panel
            for k in range(j + 1, nblocks):
                a, b = n * k, n * (k + 1)
                work[a:b, a:] -= dot_full(panel[:, a - hi:b - hi], panel[:, a - hi:], 0, 0)
            states_ref[:, hi:] -= dot_full(solved, panel, 1, 0)


def call(body, outs, in_spaces, scratch=(), mib=40):
    return pl.pallas_call(
        body,
        out_shape=outs,
        in_specs=[pl.BlockSpec(memory_space=space) for space in in_spaces],
        out_specs=[pl.BlockSpec(memory_space=pltpu.VMEM) for _ in outs],
        scratch_shapes=list(scratch),
        compiler_params=pltpu.CompilerParams(vmem_limit_bytes=mib * 2**20),
    )


def line_places(ny, nz, nk):
    lines = []
    for fixed in range(ny):
        for k in range(nk):
            line = []
            for along in range(nz):
                y, z = (fixed, along) if k == 0 else (along, fixed)
                line.append((y * nz + z) * nk + k)
            lines.append(line)
    return lines


def ring_pairs(ny, nz, nk, step):
    pairs = []
    for y in range(ny):
        for z in range(nz):
            for k in range(nk):
                to_y, to_z = ((y + step) % ny, z) if k == 0 else (y, (z + step) % nz)
                pairs.append(((y * nz + z) * nk + k, (to_y * nz + to_z) * nk + k))
    return pairs


def gather_states(vectors):
    axes = ("y", "z", "k")
    sizes = tuple(lax.axis_size(axis) for axis in axes)
    copies = jnp.broadcast_to(vectors[None], (sizes[1],) + vectors.shape)
    line = lax.all_to_all(copies, axes, 0, 0, axis_index_groups=line_places(*sizes), tiled=True)
    half = line.shape[0] // 2
    up, down = ring_pairs(*sizes, 1), ring_pairs(*sizes, -1)
    halves = [line[:half], line[half:]]
    above, below = [[h] for h in halves], [[h] for h in halves]
    for step in range(4):
        for at in (0, 1):
            if step < 3 or at == 0:
                above[at].append(lax.ppermute(above[at][-1], axes, up))
            if step < 3 or at == 1:
                below[at].append(lax.ppermute(below[at][-1], axes, down))
    return above[0] + below[0][:0:-1] + above[1] + below[1][:0:-1]


def where_blocks(cols, y, z, k):
    from_y, from_z = cols // 8, cols % 8
    near = jnp.where(k == 0, from_z, from_y)
    far = jnp.where(k == 0, y - from_y, z - from_z) % 8
    return near // 4 * 8 + far, near % 4


def sum_groups(ny, nz, nx, nk):
    def device(y, z, x, k):
        return ((y * nz + z) * nx + x) * nk + k

    four, same = [], []
    for y in range(ny):
        for z in range(nz):
            four.append([device(y, z, x, 0) for x in range(nx)])
    for x in range(nx):
        same.append([device(y, z, x, 0) for y in range(ny) for z in range(nz)])
        for y in range(0, ny, 2):
            for z in range(0, nz, 2):
                four.append([device(y + i, z + j, x, 1) for i in (0, 1) for j in (0, 1)])
    for i in (0, 1):
        for j in (0, 1):
            same.append([
                device(y + i, z + j, x, 1)
                for x in range(nx) for y in range(0, ny, 2) for z in range(0, nz, 2)
            ])
    return four, same


def sum_halves(value):
    axes = ("y", "z", "x", "k")
    four, same = sum_groups(*(lax.axis_size(axis) for axis in axes))

    def exchange(pieces, groups):
        return lax.all_to_all(pieces, axes, 0, 0, axis_index_groups=groups, tiled=True)

    def copies(piece, groups):
        return jnp.broadcast_to(piece[None], (len(groups[0]),) + piece.shape)

    part = exchange(value.reshape(len(four[0]), -1, value.shape[-1]), four).sum(0)
    piece = exchange(part.reshape(len(same[0]), -1), same).sum(0)
    part = exchange(copies(piece, same), same).reshape(part.shape)
    return exchange(copies(part, four), four).reshape(value.shape)


def per_device(vectors, onsite, tile_values, tile_rows, tile_cols, tile_count):
    own_rows, kstates = vectors.shape
    width = tile_values.shape[-1]
    slots = tile_values.shape[2]
    f32 = jnp.float32
    vm, sm = pltpu.VMEM, pltpu.SMEM
    halves = lax.axis_size("x")
    y, z, k = (lax.axis_index(axis) for axis in ("y", "z", "k"))

    rows = tile_rows.reshape(slots)
    source, place = where_blocks(tile_cols.reshape(slots), y, z, k)
    meta = jnp.concatenate([(rows + k) % 2 * halves + rows // 2, source, place, tile_count.reshape(1)])
    local = onsite[:, None] * vectors.astype(f32)
    buffers = gather_states(vectors)

    part = jax.ShapeDtypeStruct((halves, width, kstates), f32)
    keep, send = call(
        tile_products,
        [part, part],
        [sm, vm] + [vm] * len(buffers),
        [vm((2 * halves, width, kstates), f32)],
        24,
    )(meta, tile_values[0, 0], *buffers)
    other = lax.ppermute(send, "k", [(0, 1), (1, 0)])
    parts = lax.all_to_all(keep + other, "x", 0, 0, tiled=True)

    nblocks = kstates // width
    half = jax.ShapeDtypeStruct((nblocks * (nblocks + 1) // 4, width, width), f32)
    core = k.astype(jnp.int32).reshape(1)
    applied, own, other = call(
        gram_blocks,
        [jax.ShapeDtypeStruct((own_rows, kstates), f32), half, half],
        [sm, vm, vm],
    )(core, parts, local)
    own = sum_halves(own + lax.ppermute(other, "k", [(0, 1), (1, 0)]))
    other = lax.ppermute(own, "k", [(0, 1), (1, 0)])

    states, upper = call(
        factor_and_solve,
        [jax.ShapeDtypeStruct((own_rows, kstates), f32), jax.ShapeDtypeStruct((kstates, kstates), f32)],
        [sm, vm, vm, vm],
        [vm((kstates, kstates), f32), vm((width, width), f32)],
    )(core, own, other, applied)
    return (states, upper)


def solution(mesh):
    fine = Mesh(mesh.devices.reshape(8, 8, 4, 2), ("y", "z", "x", "k"))
    row, col = ("y", "z"), ("x", "k")
    return jax.shard_map(
        per_device,
        mesh=fine,
        in_specs=(
            P(row + col, None),
            P(row + col),
            P(row, col, None, None, None),
            P(row, col, None),
            P(row, col, None),
            P(row, col),
        ),
        out_specs=(P(row + col, None), P()),
        check_vma=False,
    )
```

```python
import functools

import jax
import jax.numpy as jnp
from jax import lax
from jax.experimental import pallas as pl
from jax.experimental.pallas import tpu as pltpu
from jax.sharding import Mesh, PartitionSpec as P

FULL = lax.Precision.HIGHEST
STRIP = 8


def dot_full(left, right, left_dim, right_dim):
    dims = (((left_dim,), (right_dim,)), ((), ()))
    return lax.dot_general(left, right, dims, precision=FULL, preferred_element_type=jnp.float32)


def tile_products(ids, first_place, based, meta_ref, tiles_ref, *refs):
    sources, out_ref = refs[:len(ids)], refs[-1]
    slots, places = tiles_ref.shape[0], out_ref.shape[0]
    if based:
        out_ref[...] = refs[-2][first_place:first_place + places]
    else:
        out_ref[...] = jnp.zeros_like(out_ref)

    def add(t, place, which, first, last):
        if last - first == 1:
            @pl.when(which == ids[first])
            def _():
                block = sources[first][meta_ref[2 * slots + t]]
                out_ref[place] += jnp.dot(tiles_ref[t], block, preferred_element_type=jnp.float32)
            return
        middle = (first + last) // 2
        pl.when(which < ids[middle])(lambda: add(t, place, which, first, middle))
        pl.when(which >= ids[middle])(lambda: add(t, place, which, middle, last))

    @pl.loop(0, meta_ref[3 * slots])
    def _(t):
        place = meta_ref[t] - first_place

        @pl.when((place >= 0) & (place < places))
        def _():
            add(t, place, meta_ref[slots + t], 0, len(ids))


def upper_pairs(nblocks):
    pairs = [(j, k) for j in range(nblocks) for k in range(j, nblocks)]
    return pairs[:len(pairs) // 2], pairs[len(pairs) // 2:]


def gram_blocks(core_ref, parts_ref, local_ref, applied_ref, own_ref, other_ref):
    n = own_ref.shape[1]
    applied = local_ref[...]
    for i in range(parts_ref.shape[0]):
        applied = applied + parts_ref[i]
    applied_ref[...] = applied
    nblocks = applied.shape[1] // n
    rows = [dot_full(applied[:, j * n:(j + 1) * n], applied[:, j * n:], 0, 0) for j in range(nblocks)]
    for core in (0, 1):
        @pl.when(core_ref[0] == core)
        def _():
            for half, pairs in enumerate(upper_pairs(nblocks)):
                target = own_ref if half == core else other_ref
                for at, (j, k) in enumerate(pairs):
                    target[at] = rows[j][:, (k - j) * n:(k - j + 1) * n]


def factor_diagonal(a_ref, inverse_ref, u_ref, base, n):
    sub = lax.broadcasted_iota(jnp.int32, (STRIP, n), 0)
    lane = lax.broadcasted_iota(jnp.int32, (STRIP, n), 1)
    strips = n // STRIP

    def spread(rows, k):
        return jnp.broadcast_to(rows[k:k + 1, :], (STRIP, n))

    rows_a = [a_ref[STRIP * i:STRIP * (i + 1), :] for i in range(strips)]
    rows_e = [jnp.where(lane == sub + STRIP * i, 1.0, 0.0) for i in range(strips)]
    for s in range(strips):
        first = STRIP * s
        here = slice(first, first + STRIP)
        cols = [jnp.broadcast_to(rows_a[s][:, first + k:first + k + 1], (STRIP, n)) for k in range(STRIP)]
        down_a, down_e = rows_a[s], rows_e[s]
        full_a, full_e = rows_a[s], rows_e[s]
        pivots = None
        for k in range(STRIP):
            pivot = spread(cols[k], k)
            recip = 1.0 / pivot
            at = sub == k
            both = jnp.where(at, -1.0, cols[k]) * recip
            below = jnp.where(sub > k, cols[k], 0.0) * recip
            for b in range(k + 1, STRIP):
                cols[b] = jnp.where(at, 0.0, cols[b]) - both * spread(cols[b], k)
            row_a, row_e = spread(full_a, k), spread(full_e, k)
            down_a = down_a - below * spread(down_a, k)
            down_e = down_e - below * spread(down_e, k)
            full_a = jnp.where(at, 0.0, full_a) - both * row_a
            full_e = jnp.where(at, 0.0, full_e) - both * row_e
            pivots = pivot if pivots is None else jnp.where(sub >= k, pivot, pivots)
        scale = lax.rsqrt(pivots)
        u_ref[base + first:base + first + STRIP, base:base + n] = jnp.where(lane >= sub + first, down_a * scale, 0.0)
        inverse_ref[here, :] = down_e * scale
        spread_a = [spread(full_a, k) for k in range(STRIP)]
        spread_e = [spread(full_e, k) for k in range(STRIP)]
        for i in range(s + 1, strips):
            next_a, next_e = rows_a[i], rows_e[i]
            for k in range(STRIP):
                c = jnp.broadcast_to(rows_a[i][:, first + k:first + k + 1], (STRIP, n))
                next_a = next_a - c * spread_a[k]
                next_e = next_e - c * spread_e[k]
            rows_a[i], rows_e[i] = next_a, next_e


def factor_and_solve(core_ref, own_ref, other_ref, applied_ref, states_ref, u_ref, work, inverse):
    n = own_ref.shape[1]
    size = u_ref.shape[0]
    nblocks = size // n
    for core in (0, 1):
        @pl.when(core_ref[0] == core)
        def _():
            for half, pairs in enumerate(upper_pairs(nblocks)):
                source = own_ref if half == core else other_ref
                for at, (j, k) in enumerate(pairs):
                    work[n * j:n * (j + 1), n * k:n * (k + 1)] = source[at]
    states_ref[...] = applied_ref[...]
    u_ref[...] = jnp.zeros_like(u_ref)
    for j in range(nblocks):
        lo, hi = n * j, n * (j + 1)
        factor_diagonal(work.at[lo:hi, lo:hi], inverse, u_ref, lo, n)
        inv = inverse[...]
        solved = dot_full(states_ref[:, lo:hi], inv, 1, 1)
        states_ref[:, lo:hi] = solved
        if hi < size:
            panel = dot_full(inv, work[lo:hi, hi:], 1, 0)
            u_ref[lo:hi, hi:] = panel
            for k in range(j + 1, nblocks):
                a, b = n * k, n * (k + 1)
                work[a:b, a:] -= dot_full(panel[:, a - hi:b - hi], panel[:, a - hi:], 0, 0)
            states_ref[:, hi:] -= dot_full(solved, panel, 1, 0)


def call(body, outs, in_spaces, scratch=(), mib=40):
    return pl.pallas_call(
        body,
        out_shape=outs,
        in_specs=[pl.BlockSpec(memory_space=space) for space in in_spaces],
        out_specs=[pl.BlockSpec(memory_space=pltpu.VMEM) for _ in outs],
        scratch_shapes=list(scratch),
        compiler_params=pltpu.CompilerParams(vmem_limit_bytes=mib * 2**20),
    )


def line_places(ny, nz, nk):
    lines = []
    for fixed in range(ny):
        for k in range(nk):
            line = []
            for along in range(nz):
                y, z = (fixed, along) if k == 0 else (along, fixed)
                line.append((y * nz + z) * nk + k)
            lines.append(line)
    return lines


def ring_pairs(ny, nz, nk, step):
    pairs = []
    for y in range(ny):
        for z in range(nz):
            for k in range(nk):
                to_y, to_z = ((y + step) % ny, z) if k == 0 else (y, (z + step) % nz)
                pairs.append(((y * nz + z) * nk + k, (to_y * nz + to_z) * nk + k))
    return pairs


def gather_states(vectors):
    axes = ("y", "z", "k")
    sizes = tuple(lax.axis_size(axis) for axis in axes)
    copies = jnp.broadcast_to(vectors[None], (sizes[1],) + vectors.shape)
    line = lax.all_to_all(copies, axes, 0, 0, axis_index_groups=line_places(*sizes), tiled=True)
    half = line.shape[0] // 2
    up, down = ring_pairs(*sizes, 1), ring_pairs(*sizes, -1)
    halves = [line[:half], line[half:]]
    above, below = [[h] for h in halves], [[h] for h in halves]
    for step in range(4):
        for at in (0, 1):
            if step < 3 or at == 0:
                above[at].append(lax.ppermute(above[at][-1], axes, up))
            if step < 3 or at == 1:
                below[at].append(lax.ppermute(below[at][-1], axes, down))
    return above[0] + below[0][:0:-1] + above[1] + below[1][:0:-1]


def where_blocks(cols, y, z, k):
    from_y, from_z = cols // 8, cols % 8
    near = jnp.where(k == 0, from_z, from_y)
    far = jnp.where(k == 0, y - from_y, z - from_z) % 8
    return near // 4 * 8 + far, near % 4


def sum_groups(ny, nz, nx, nk):
    def device(y, z, x, k):
        return ((y * nz + z) * nx + x) * nk + k

    four, same = [], []
    for y in range(ny):
        for z in range(nz):
            four.append([device(y, z, x, 0) for x in range(nx)])
    for x in range(nx):
        same.append([device(y, z, x, 0) for y in range(ny) for z in range(nz)])
        for y in range(0, ny, 2):
            for z in range(0, nz, 2):
                four.append([device(y + i, z + j, x, 1) for i in (0, 1) for j in (0, 1)])
    for i in (0, 1):
        for j in (0, 1):
            same.append([
                device(y + i, z + j, x, 1)
                for x in range(nx) for y in range(0, ny, 2) for z in range(0, nz, 2)
            ])
    return four, same


def sum_halves(value):
    axes = ("y", "z", "x", "k")
    four, same = sum_groups(*(lax.axis_size(axis) for axis in axes))

    def exchange(pieces, groups):
        return lax.all_to_all(pieces, axes, 0, 0, axis_index_groups=groups, tiled=True)

    def copies(piece, groups):
        return jnp.broadcast_to(piece[None], (len(groups[0]),) + piece.shape)

    part = exchange(value.reshape(len(four[0]), -1, value.shape[-1]), four).sum(0)
    piece = exchange(part.reshape(len(same[0]), -1), same).sum(0)
    part = exchange(copies(piece, same), same).reshape(part.shape)
    return exchange(copies(part, four), four).reshape(value.shape)


def per_device(vectors, onsite, tile_values, tile_rows, tile_cols, tile_count):
    own_rows, kstates = vectors.shape
    width = tile_values.shape[-1]
    slots = tile_values.shape[2]
    f32 = jnp.float32
    vm, sm = pltpu.VMEM, pltpu.SMEM
    halves = lax.axis_size("x")
    y, z, k = (lax.axis_index(axis) for axis in ("y", "z", "k"))

    rows = tile_rows.reshape(slots)
    source, place = where_blocks(tile_cols.reshape(slots), y, z, k)
    meta = jnp.concatenate([(rows + k) % 2 * halves + rows // 2, source, place, tile_count.reshape(1)])
    local = onsite[:, None] * vectors.astype(f32)
    buffers = gather_states(vectors)

    tiles = tile_values[0, 0]
    late = [4, 5, 11, 12]
    early = [at for at in range(len(buffers)) if at not in late]

    def products(ids, first_place, places, *base):
        return call(
            functools.partial(tile_products, ids, first_place, bool(base)),
            [jax.ShapeDtypeStruct((places, width, kstates), f32)],
            [sm, vm] + [vm] * (len(ids) + len(base)),
            (),
            24,
        )(meta, tiles, *[buffers[at] for at in ids], *base)[0]

    sums = products(early, 0, 2 * halves)
    send = products(late, halves, halves, sums)
    other = lax.ppermute(send, "k", [(0, 1), (1, 0)])
    keep = products(late, 0, halves, sums)
    parts = lax.all_to_all(keep + other, "x", 0, 0, tiled=True)

    nblocks = kstates // width
    half = jax.ShapeDtypeStruct((nblocks * (nblocks + 1) // 4, width, width), f32)
    core = k.astype(jnp.int32).reshape(1)
    applied, own, other = call(
        gram_blocks,
        [jax.ShapeDtypeStruct((own_rows, kstates), f32), half, half],
        [sm, vm, vm],
    )(core, parts, local)
    own = sum_halves(own + lax.ppermute(other, "k", [(0, 1), (1, 0)]))
    other = lax.ppermute(own, "k", [(0, 1), (1, 0)])

    states, upper = call(
        factor_and_solve,
        [jax.ShapeDtypeStruct((own_rows, kstates), f32), jax.ShapeDtypeStruct((kstates, kstates), f32)],
        [sm, vm, vm, vm],
        [vm((kstates, kstates), f32), vm((width, width), f32)],
    )(core, own, other, applied)
    return (states, upper)


def solution(mesh):
    fine = Mesh(mesh.devices.reshape(8, 8, 4, 2), ("y", "z", "x", "k"))
    row, col = ("y", "z"), ("x", "k")
    return jax.shard_map(
        per_device,
        mesh=fine,
        in_specs=(
            P(row + col, None),
            P(row + col),
            P(row, col, None, None, None),
            P(row, col, None),
            P(row, col, None),
            P(row, col),
        ),
        out_specs=(P(row + col, None), P()),
        check_vma=False,
    )
```

```python
import functools

import jax
import jax.numpy as jnp
from jax import lax
from jax.experimental import pallas as pl
from jax.experimental.pallas import tpu as pltpu
from jax.sharding import Mesh, PartitionSpec as P

FULL = lax.Precision.HIGHEST
STRIP = 8


def dot_full(left, right, left_dim, right_dim):
    dims = (((left_dim,), (right_dim,)), ((), ()))
    return lax.dot_general(left, right, dims, precision=FULL, preferred_element_type=jnp.float32)


def tile_products(ids, first_place, based, meta_ref, tiles_ref, *refs):
    sources, out_ref = refs[:len(ids)], refs[-1]
    slots, places = tiles_ref.shape[0], out_ref.shape[0]
    if based:
        out_ref[...] = refs[-2][first_place:first_place + places]
    else:
        out_ref[...] = jnp.zeros_like(out_ref)

    def add(t, place, which, first, last):
        if last - first == 1:
            @pl.when(which == ids[first])
            def _():
                block = sources[first][meta_ref[2 * slots + t]]
                out_ref[place] += jnp.dot(tiles_ref[t], block, preferred_element_type=jnp.float32)
            return
        middle = (first + last) // 2
        pl.when(which < ids[middle])(lambda: add(t, place, which, first, middle))
        pl.when(which >= ids[middle])(lambda: add(t, place, which, middle, last))

    @pl.loop(0, meta_ref[3 * slots])
    def _(t):
        place = meta_ref[t] - first_place

        @pl.when((place >= 0) & (place < places))
        def _():
            add(t, place, meta_ref[slots + t], 0, len(ids))


def upper_pairs(nblocks):
    return [(j, k) for j in range(nblocks) for k in range(j, nblocks)]


def gram_blocks(parts_ref, local_ref, applied_ref, gram_ref):
    n = gram_ref.shape[1]
    applied = local_ref[...]
    for i in range(parts_ref.shape[0]):
        applied = applied + parts_ref[i]
    applied_ref[...] = applied
    nblocks = applied.shape[1] // n
    rows = [dot_full(applied[:, j * n:(j + 1) * n], applied[:, j * n:], 0, 0) for j in range(nblocks)]
    for at, (j, k) in enumerate(upper_pairs(nblocks)):
        gram_ref[at] = rows[j][:, (k - j) * n:(k - j + 1) * n]


def three_parts(value):
    high = value.astype(jnp.bfloat16)
    rest = value - high.astype(jnp.float32)
    middle = rest.astype(jnp.bfloat16)
    return high, middle, (rest - middle.astype(jnp.float32)).astype(jnp.bfloat16)


def dot_few_rows(left, right):
    h, m, l = three_parts(left)
    high, middle, low = three_parts(right)
    stacked = jnp.concatenate([h, h, m, h, m, l]), jnp.concatenate([high, middle, high, low, middle, high])
    return lax.dot_general(*stacked, (((0,), (0,)), ((), ())), preferred_element_type=jnp.float32)


def factor_diagonal(a_ref, inverse_ref, u_ref, base, n):
    sub = lax.broadcasted_iota(jnp.int32, (STRIP, n), 0)
    lane = lax.broadcasted_iota(jnp.int32, (STRIP, n), 1)
    strips = n // STRIP

    def spread(rows, k):
        return jnp.broadcast_to(rows[k:k + 1, :], (STRIP, n))

    rows_a = [a_ref[STRIP * i:STRIP * (i + 1), :] for i in range(strips)]
    rows_e = [jnp.where(lane == sub + STRIP * i, 1.0, 0.0) for i in range(strips)]
    for s in range(strips):
        first = STRIP * s
        here = slice(first, first + STRIP)
        cols = [jnp.broadcast_to(rows_a[s][:, first + k:first + k + 1], (STRIP, n)) for k in range(STRIP)]
        down_a, down_e = rows_a[s], rows_e[s]
        full_a, full_e = rows_a[s], rows_e[s]
        pivots = None
        for k in range(STRIP):
            pivot = spread(cols[k], k)
            recip = 1.0 / pivot
            at = sub == k
            both = jnp.where(at, -1.0, cols[k]) * recip
            below = jnp.where(sub > k, cols[k], 0.0) * recip
            for b in range(k + 1, STRIP):
                cols[b] = jnp.where(at, 0.0, cols[b]) - both * spread(cols[b], k)
            row_a, row_e = spread(full_a, k), spread(full_e, k)
            down_a = down_a - below * spread(down_a, k)
            down_e = down_e - below * spread(down_e, k)
            full_a = jnp.where(at, 0.0, full_a) - both * row_a
            full_e = jnp.where(at, 0.0, full_e) - both * row_e
            pivots = pivot if pivots is None else jnp.where(sub >= k, pivot, pivots)
        scale = lax.rsqrt(pivots)
        u_ref[base + first:base + first + STRIP, base:base + n] = jnp.where(lane >= sub + first, down_a * scale, 0.0)
        inverse_ref[here, :] = down_e * scale
        if s + 1 < strips:
            here_a = rows_a[s]
            for k in range(STRIP):
                c = jnp.broadcast_to(rows_a[s + 1][:, first + k:first + k + 1], (STRIP, n))
                taken_a = c * spread(full_a, k) + (taken_a if k else 0.0)
                taken_e = c * spread(full_e, k) + (taken_e if k else 0.0)
            rows_a[s + 1], rows_e[s + 1] = rows_a[s + 1] - taken_a, rows_e[s + 1] - taken_e
        if s + 2 < strips:
            taken = dot_few_rows(here_a, jnp.concatenate([full_a, full_e], axis=1))
            for i in range(s + 2, strips):
                rows_a[i] = rows_a[i] - taken[STRIP * i:STRIP * (i + 1), :n]
                rows_e[i] = rows_e[i] - taken[STRIP * i:STRIP * (i + 1), n:]


def factor_and_solve(gram_ref, applied_ref, states_ref, u_ref, work, inverse):
    n = gram_ref.shape[1]
    size = u_ref.shape[0]
    nblocks = size // n
    for at, (j, k) in enumerate(upper_pairs(nblocks)):
        work[n * j:n * (j + 1), n * k:n * (k + 1)] = gram_ref[at]
    states_ref[...] = applied_ref[...]
    u_ref[...] = jnp.zeros_like(u_ref)
    for j in range(nblocks):
        lo, hi = n * j, n * (j + 1)
        factor_diagonal(work.at[lo:hi, lo:hi], inverse, u_ref, lo, n)
        inv = inverse[...]
        solved = dot_full(states_ref[:, lo:hi], inv, 1, 1)
        states_ref[:, lo:hi] = solved
        if hi < size:
            panel = dot_full(inv, work[lo:hi, hi:], 1, 0)
            u_ref[lo:hi, hi:] = panel
            for k in range(j + 1, nblocks):
                a, b = n * k, n * (k + 1)
                work[a:b, a:] -= dot_full(panel[:, a - hi:b - hi], panel[:, a - hi:], 0, 0)
            states_ref[:, hi:] -= dot_full(solved, panel, 1, 0)


def call(body, outs, in_spaces, scratch=(), mib=40):
    return pl.pallas_call(
        body,
        out_shape=outs,
        in_specs=[pl.BlockSpec(memory_space=space) for space in in_spaces],
        out_specs=[pl.BlockSpec(memory_space=pltpu.VMEM) for _ in outs],
        scratch_shapes=list(scratch),
        compiler_params=pltpu.CompilerParams(vmem_limit_bytes=mib * 2**20),
    )


def line_places(ny, nz, nk):
    lines = []
    for fixed in range(ny):
        for k in range(nk):
            line = []
            for along in range(nz):
                y, z = (fixed, along) if k == 0 else (along, fixed)
                line.append((y * nz + z) * nk + k)
            lines.append(line)
    return lines


def ring_pairs(ny, nz, nk, step):
    pairs = []
    for y in range(ny):
        for z in range(nz):
            for k in range(nk):
                to_y, to_z = ((y + step) % ny, z) if k == 0 else (y, (z + step) % nz)
                pairs.append(((y * nz + z) * nk + k, (to_y * nz + to_z) * nk + k))
    return pairs


def gather_states(vectors):
    axes = ("y", "z", "k")
    sizes = tuple(lax.axis_size(axis) for axis in axes)
    copies = jnp.broadcast_to(vectors[None], (sizes[1],) + vectors.shape)
    line = lax.all_to_all(copies, axes, 0, 0, axis_index_groups=line_places(*sizes), tiled=True)
    half = line.shape[0] // 2
    up, down = ring_pairs(*sizes, 1), ring_pairs(*sizes, -1)
    halves = [line[:half], line[half:]]
    above, below = [[h] for h in halves], [[h] for h in halves]
    for step in range(4):
        for at in (0, 1):
            if step < 3 or at == 0:
                above[at].append(lax.ppermute(above[at][-1], axes, up))
            if step < 3 or at == 1:
                below[at].append(lax.ppermute(below[at][-1], axes, down))
    return above[0] + below[0][:0:-1] + above[1] + below[1][:0:-1]


def where_blocks(cols, y, z, k):
    from_y, from_z = cols // 8, cols % 8
    near = jnp.where(k == 0, from_z, from_y)
    far = jnp.where(k == 0, y - from_y, z - from_z) % 8
    return near // 4 * 8 + far, near % 4


def sum_groups(ny, nz, nx, nk):
    def device(y, z, x, k):
        return ((y * nz + z) * nx + x) * nk + k

    four, same = [], []
    for y in range(ny):
        for z in range(nz):
            four.append([device(y, z, x, 0) for x in range(nx)])
    for x in range(nx):
        same.append([device(y, z, x, 0) for y in range(ny) for z in range(nz)])
        for y in range(0, ny, 2):
            for z in range(0, nz, 2):
                four.append([device(y + i, z + j, x, 1) for i in (0, 1) for j in (0, 1)])
    for i in (0, 1):
        for j in (0, 1):
            same.append([
                device(y + i, z + j, x, 1)
                for x in range(nx) for y in range(0, ny, 2) for z in range(0, nz, 2)
            ])
    return four, same


def sum_halves(value):
    axes = ("y", "z", "x", "k")
    four, same = sum_groups(*(lax.axis_size(axis) for axis in axes))

    def exchange(pieces, groups):
        return lax.all_to_all(pieces, axes, 0, 0, axis_index_groups=groups, tiled=True)

    def copies(piece, groups):
        return jnp.broadcast_to(piece[None], (len(groups[0]),) + piece.shape)

    part = exchange(value.reshape(len(four[0]), -1, value.shape[-1]), four).sum(0)
    piece = exchange(part.reshape(len(same[0]), -1), same).sum(0)
    part = exchange(copies(piece, same), same).reshape(part.shape)
    return exchange(copies(part, four), four).reshape(value.shape)


def per_device(vectors, onsite, tile_values, tile_rows, tile_cols, tile_count):
    own_rows, kstates = vectors.shape
    width = tile_values.shape[-1]
    slots = tile_values.shape[2]
    f32 = jnp.float32
    vm, sm = pltpu.VMEM, pltpu.SMEM
    halves = lax.axis_size("x")
    y, z, k = (lax.axis_index(axis) for axis in ("y", "z", "k"))

    rows = tile_rows.reshape(slots)
    source, place = where_blocks(tile_cols.reshape(slots), y, z, k)
    meta = jnp.concatenate([(rows + k) % 2 * halves + rows // 2, source, place, tile_count.reshape(1)])
    local = onsite[:, None] * vectors.astype(f32)
    buffers = gather_states(vectors)

    tiles = tile_values[0, 0]
    late = [4, 5, 11, 12]
    early = [at for at in range(len(buffers)) if at not in late]

    def products(ids, first_place, places, *base):
        return call(
            functools.partial(tile_products, ids, first_place, bool(base)),
            [jax.ShapeDtypeStruct((places, width, kstates), f32)],
            [sm, vm] + [vm] * (len(ids) + len(base)),
            (),
            24,
        )(meta, tiles, *[buffers[at] for at in ids], *base)[0]

    sums = products(early, 0, 2 * halves)
    send = products(late, halves, halves, sums)
    other = lax.ppermute(send, "k", [(0, 1), (1, 0)])
    keep = products(late, 0, halves, sums)
    parts = lax.all_to_all(keep + other, "x", 0, 0, tiled=True)

    nblocks = kstates // width
    blocks = nblocks * (nblocks + 1) // 2
    applied, gram = call(
        gram_blocks,
        [jax.ShapeDtypeStruct((own_rows, kstates), f32), jax.ShapeDtypeStruct((blocks, width, width), f32)],
        [vm, vm],
    )(parts, local)
    cores = lax.axis_size("k")
    halves_of_gram = gram.reshape((cores, blocks // cores) + gram.shape[1:])
    half = sum_halves(lax.all_to_all(halves_of_gram, "k", 0, 0, tiled=True).sum(0))
    both = jnp.broadcast_to(half[None], (cores,) + half.shape)
    gram = lax.all_to_all(both, "k", 0, 0, tiled=True).reshape(gram.shape)

    states, upper = call(
        factor_and_solve,
        [jax.ShapeDtypeStruct((own_rows, kstates), f32), jax.ShapeDtypeStruct((kstates, kstates), f32)],
        [vm, vm],
        [vm((kstates, kstates), f32), vm((width, width), f32)],
    )(gram, applied)
    return (states, upper)


def solution(mesh):
    fine = Mesh(mesh.devices.reshape(8, 8, 4, 2), ("y", "z", "x", "k"))
    row, col = ("y", "z"), ("x", "k")
    return jax.shard_map(
        per_device,
        mesh=fine,
        in_specs=(
            P(row + col, None),
            P(row + col),
            P(row, col, None, None, None),
            P(row, col, None),
            P(row, col, None),
            P(row, col),
        ),
        out_specs=(P(row + col, None), P()),
        check_vma=False,
    )
```

```python
import functools

import jax
import jax.numpy as jnp
from jax import lax
from jax.experimental import pallas as pl
from jax.experimental.pallas import tpu as pltpu
from jax.sharding import Mesh, PartitionSpec as P

FULL = lax.Precision.HIGHEST
STRIP = 16


def dot_full(left, right, left_dim, right_dim):
    dims = (((left_dim,), (right_dim,)), ((), ()))
    return lax.dot_general(left, right, dims, precision=FULL, preferred_element_type=jnp.float32)


def tile_products(ids, first_place, based, meta_ref, tiles_ref, *refs):
    sources, out_ref = refs[:len(ids)], refs[-1]
    slots, places = tiles_ref.shape[0], out_ref.shape[0]
    if based:
        out_ref[...] = refs[-2][first_place:first_place + places]
    else:
        out_ref[...] = jnp.zeros_like(out_ref)

    def add(t, place, which, first, last):
        if last - first == 1:
            @pl.when(which == ids[first])
            def _():
                block = sources[first][meta_ref[2 * slots + t]]
                out_ref[place] += jnp.dot(tiles_ref[t], block, preferred_element_type=jnp.float32)
            return
        middle = (first + last) // 2
        pl.when(which < ids[middle])(lambda: add(t, place, which, first, middle))
        pl.when(which >= ids[middle])(lambda: add(t, place, which, middle, last))

    @pl.loop(0, meta_ref[3 * slots])
    def _(t):
        place = meta_ref[t] - first_place

        @pl.when((place >= 0) & (place < places))
        def _():
            add(t, place, meta_ref[slots + t], 0, len(ids))


def upper_pairs(nblocks):
    pairs = [(j, k) for j in range(nblocks) for k in range(j, nblocks)]
    return pairs[:len(pairs) // 2], pairs[len(pairs) // 2:]


def gram_blocks(core_ref, parts_ref, local_ref, applied_ref, own_ref, other_ref):
    n = own_ref.shape[1]
    applied = local_ref[...]
    for i in range(parts_ref.shape[0]):
        applied = applied + parts_ref[i]
    applied_ref[...] = applied
    nblocks = applied.shape[1] // n
    rows = [dot_full(applied[:, j * n:(j + 1) * n], applied[:, j * n:], 0, 0) for j in range(nblocks)]
    for core in (0, 1):
        @pl.when(core_ref[0] == core)
        def _():
            for half, pairs in enumerate(upper_pairs(nblocks)):
                target = own_ref if half == core else other_ref
                for at, (j, k) in enumerate(pairs):
                    target[at] = rows[j][:, (k - j) * n:(k - j + 1) * n]


def three_parts(value):
    high = value.astype(jnp.bfloat16)
    rest = value - high.astype(jnp.float32)
    middle = rest.astype(jnp.bfloat16)
    return high, middle, (rest - middle.astype(jnp.float32)).astype(jnp.bfloat16)


def dot_few_rows(left, right):
    h, m, l = three_parts(left)
    high, middle, low = three_parts(right)
    stacked = jnp.concatenate([h, h, m, h, m, l]), jnp.concatenate([high, middle, high, low, middle, high])
    return lax.dot_general(*stacked, (((0,), (0,)), ((), ())), preferred_element_type=jnp.float32)


def factor_diagonal(a_ref, inverse_ref, u_ref, base, n):
    sub = lax.broadcasted_iota(jnp.int32, (STRIP, n), 0)
    lane = lax.broadcasted_iota(jnp.int32, (STRIP, n), 1)
    strips = n // STRIP

    def spread(rows, k):
        return jnp.broadcast_to(rows[k:k + 1, :], (STRIP, n))

    rows_a = [a_ref[STRIP * i:STRIP * (i + 1), :] for i in range(strips)]
    rows_e = [jnp.where(lane == sub + STRIP * i, 1.0, 0.0) for i in range(strips)]
    for s in range(strips):
        first = STRIP * s
        here = slice(first, first + STRIP)
        cols = [jnp.broadcast_to(rows_a[s][:, first + k:first + k + 1], (STRIP, n)) for k in range(STRIP)]
        down_a, down_e = rows_a[s], rows_e[s]
        full_a, full_e = rows_a[s], rows_e[s]
        pivots = None
        for k in range(STRIP):
            pivot = spread(cols[k], k)
            recip = 1.0 / pivot
            at = sub == k
            both = jnp.where(at, -1.0, cols[k]) * recip
            below = jnp.where(sub > k, cols[k], 0.0) * recip
            for b in range(k + 1, STRIP):
                cols[b] = jnp.where(at, 0.0, cols[b]) - both * spread(cols[b], k)
            row_a, row_e = spread(full_a, k), spread(full_e, k)
            down_a = down_a - below * spread(down_a, k)
            down_e = down_e - below * spread(down_e, k)
            full_a = jnp.where(at, 0.0, full_a) - both * row_a
            full_e = jnp.where(at, 0.0, full_e) - both * row_e
            pivots = pivot if pivots is None else jnp.where(sub >= k, pivot, pivots)
        scale = lax.rsqrt(pivots)
        u_ref[base + first:base + first + STRIP, base:base + n] = jnp.where(lane >= sub + first, down_a * scale, 0.0)
        inverse_ref[here, :] = down_e * scale
        if s + 1 < strips:
            here_a = rows_a[s]
            for k in range(STRIP):
                c = jnp.broadcast_to(rows_a[s + 1][:, first + k:first + k + 1], (STRIP, n))
                taken_a = c * spread(full_a, k) + (taken_a if k else 0.0)
                taken_e = c * spread(full_e, k) + (taken_e if k else 0.0)
            rows_a[s + 1], rows_e[s + 1] = rows_a[s + 1] - taken_a, rows_e[s + 1] - taken_e
        if s + 2 < strips:
            taken = dot_few_rows(here_a, jnp.concatenate([full_a, full_e], axis=1))
            for i in range(s + 2, strips):
                rows_a[i] = rows_a[i] - taken[STRIP * i:STRIP * (i + 1), :n]
                rows_e[i] = rows_e[i] - taken[STRIP * i:STRIP * (i + 1), n:]


def factor_and_solve(gram_ref, applied_ref, states_ref, u_ref, work, inverse):
    n = gram_ref.shape[1]
    size = u_ref.shape[0]
    nblocks = size // n
    for at, (j, k) in enumerate(sum(upper_pairs(nblocks), [])):
        work[n * j:n * (j + 1), n * k:n * (k + 1)] = gram_ref[at]
    states_ref[...] = applied_ref[...]
    u_ref[...] = jnp.zeros_like(u_ref)
    for j in range(nblocks):
        lo, hi = n * j, n * (j + 1)
        factor_diagonal(work.at[lo:hi, lo:hi], inverse, u_ref, lo, n)
        inv = inverse[...]
        solved = dot_full(states_ref[:, lo:hi], inv, 1, 1)
        states_ref[:, lo:hi] = solved
        if hi < size:
            panel = dot_full(inv, work[lo:hi, hi:], 1, 0)
            u_ref[lo:hi, hi:] = panel
            for k in range(j + 1, nblocks):
                a, b = n * k, n * (k + 1)
                work[a:b, a:] -= dot_full(panel[:, a - hi:b - hi], panel[:, a - hi:], 0, 0)
            states_ref[:, hi:] -= dot_full(solved, panel, 1, 0)


def call(body, outs, in_spaces, scratch=(), mib=40):
    return pl.pallas_call(
        body,
        out_shape=outs,
        in_specs=[pl.BlockSpec(memory_space=space) for space in in_spaces],
        out_specs=[pl.BlockSpec(memory_space=pltpu.VMEM) for _ in outs],
        scratch_shapes=list(scratch),
        compiler_params=pltpu.CompilerParams(vmem_limit_bytes=mib * 2**20),
    )


def line_places(ny, nz, nk):
    lines = []
    for fixed in range(ny):
        for k in range(nk):
            line = []
            for along in range(nz):
                y, z = (fixed, along) if k == 0 else (along, fixed)
                line.append((y * nz + z) * nk + k)
            lines.append(line)
    return lines


def ring_pairs(ny, nz, nk, step):
    pairs = []
    for y in range(ny):
        for z in range(nz):
            for k in range(nk):
                to_y, to_z = ((y + step) % ny, z) if k == 0 else (y, (z + step) % nz)
                pairs.append(((y * nz + z) * nk + k, (to_y * nz + to_z) * nk + k))
    return pairs


def gather_states(vectors):
    axes = ("y", "z", "k")
    sizes = tuple(lax.axis_size(axis) for axis in axes)
    copies = jnp.broadcast_to(vectors[None], (sizes[1],) + vectors.shape)
    line = lax.all_to_all(copies, axes, 0, 0, axis_index_groups=line_places(*sizes), tiled=True)
    half = line.shape[0] // 2
    up, down = ring_pairs(*sizes, 1), ring_pairs(*sizes, -1)
    halves = [line[:half], line[half:]]
    above, below = [[h] for h in halves], [[h] for h in halves]
    for step in range(4):
        for at in (0, 1):
            if step < 3 or at == 0:
                above[at].append(lax.ppermute(above[at][-1], axes, up))
            if step < 3 or at == 1:
                below[at].append(lax.ppermute(below[at][-1], axes, down))
    return above[0] + below[0][:0:-1] + above[1] + below[1][:0:-1]


def where_blocks(cols, y, z, k):
    from_y, from_z = cols // 8, cols % 8
    near = jnp.where(k == 0, from_z, from_y)
    far = jnp.where(k == 0, y - from_y, z - from_z) % 8
    return near // 4 * 8 + far, near % 4


def sum_groups(ny, nz, nx, nk):
    def device(y, z, x, k):
        return ((y * nz + z) * nx + x) * nk + k

    four, same = [], []
    for y in range(ny):
        for z in range(nz):
            four.append([device(y, z, x, 0) for x in range(nx)])
    for x in range(nx):
        same.append([device(y, z, x, 0) for y in range(ny) for z in range(nz)])
        for y in range(0, ny, 2):
            for z in range(0, nz, 2):
                four.append([device(y + i, z + j, x, 1) for i in (0, 1) for j in (0, 1)])
    for i in (0, 1):
        for j in (0, 1):
            same.append([
                device(y + i, z + j, x, 1)
                for x in range(nx) for y in range(0, ny, 2) for z in range(0, nz, 2)
            ])
    return four, same


def sum_halves(value):
    axes = ("y", "z", "x", "k")
    four, same = sum_groups(*(lax.axis_size(axis) for axis in axes))

    def exchange(pieces, groups):
        return lax.all_to_all(pieces, axes, 0, 0, axis_index_groups=groups, tiled=True)

    def copies(piece, groups):
        return jnp.broadcast_to(piece[None], (len(groups[0]),) + piece.shape)

    part = exchange(value.reshape(len(four[0]), -1, value.shape[-1]), four).sum(0)
    piece = exchange(part.reshape(len(same[0]), -1), same).sum(0)
    part = exchange(copies(piece, same), same).reshape(part.shape)
    return exchange(copies(part, four), four).reshape(value.shape)


def per_device(vectors, onsite, tile_values, tile_rows, tile_cols, tile_count):
    own_rows, kstates = vectors.shape
    width = tile_values.shape[-1]
    slots = tile_values.shape[2]
    f32 = jnp.float32
    vm, sm = pltpu.VMEM, pltpu.SMEM
    halves = lax.axis_size("x")
    y, z, k = (lax.axis_index(axis) for axis in ("y", "z", "k"))

    rows = tile_rows.reshape(slots)
    source, place = where_blocks(tile_cols.reshape(slots), y, z, k)
    meta = jnp.concatenate([(rows + k) % 2 * halves + rows // 2, source, place, tile_count.reshape(1)])
    local = onsite[:, None] * vectors.astype(f32)
    buffers = gather_states(vectors)

    tiles = tile_values[0, 0]
    late = [4, 5, 11, 12]
    early = [at for at in range(len(buffers)) if at not in late]

    def products(ids, first_place, places, *base):
        return call(
            functools.partial(tile_products, ids, first_place, bool(base)),
            [jax.ShapeDtypeStruct((places, width, kstates), f32)],
            [sm, vm] + [vm] * (len(ids) + len(base)),
            (),
            24,
        )(meta, tiles, *[buffers[at] for at in ids], *base)[0]

    sums = products(early, 0, 2 * halves)
    send = products(late, halves, halves, sums)
    other = lax.ppermute(send, "k", [(0, 1), (1, 0)])
    keep = products(late, 0, halves, sums)
    parts = lax.all_to_all(keep + other, "x", 0, 0, tiled=True)

    nblocks = kstates // width
    half = jax.ShapeDtypeStruct((nblocks * (nblocks + 1) // 4, width, width), f32)
    applied, own, other = call(
        gram_blocks,
        [jax.ShapeDtypeStruct((own_rows, kstates), f32), half, half],
        [sm, vm, vm],
    )(k.astype(jnp.int32).reshape(1), parts, local)
    own = sum_halves(own + lax.ppermute(other, "k", [(0, 1), (1, 0)]))
    gram = lax.all_gather(own, "k", axis=0, tiled=True)

    states, upper = call(
        factor_and_solve,
        [jax.ShapeDtypeStruct((own_rows, kstates), f32), jax.ShapeDtypeStruct((kstates, kstates), f32)],
        [vm, vm],
        [vm((kstates, kstates), f32), vm((width, width), f32)],
    )(gram, applied)
    return (states, upper)


def solution(mesh):
    fine = Mesh(mesh.devices.reshape(8, 8, 4, 2), ("y", "z", "x", "k"))
    row, col = ("y", "z"), ("x", "k")
    return jax.shard_map(
        per_device,
        mesh=fine,
        in_specs=(
            P(row + col, None),
            P(row + col),
            P(row, col, None, None, None),
            P(row, col, None),
            P(row, col, None),
            P(row, col),
        ),
        out_specs=(P(row + col, None), P()),
        check_vma=False,
    )
```

```python
import functools

import jax
import jax.numpy as jnp
from jax import lax
from jax.experimental import pallas as pl
from jax.experimental.pallas import tpu as pltpu
from jax.sharding import Mesh, PartitionSpec as P

FULL = lax.Precision.HIGHEST
STRIP = 16


def dot_full(left, right, left_dim, right_dim):
    dims = (((left_dim,), (right_dim,)), ((), ()))
    return lax.dot_general(left, right, dims, precision=FULL, preferred_element_type=jnp.float32)


def tile_products(ids, first_place, based, meta_ref, tiles_ref, *refs):
    sources, out_ref = refs[:len(ids)], refs[-1]
    slots, places = tiles_ref.shape[0], out_ref.shape[0]
    if based:
        out_ref[...] = refs[-2][first_place:first_place + places]
    else:
        out_ref[...] = jnp.zeros_like(out_ref)

    def add(t, place, which, first, last):
        if last - first == 1:
            @pl.when(which == ids[first])
            def _():
                block = sources[first][meta_ref[2 * slots + t]]
                out_ref[place] += jnp.dot(tiles_ref[t], block, preferred_element_type=jnp.float32)
            return
        middle = (first + last) // 2
        pl.when(which < ids[middle])(lambda: add(t, place, which, first, middle))
        pl.when(which >= ids[middle])(lambda: add(t, place, which, middle, last))

    @pl.loop(0, meta_ref[3 * slots])
    def _(t):
        place = meta_ref[t] - first_place

        @pl.when((place >= 0) & (place < places))
        def _():
            add(t, place, meta_ref[slots + t], 0, len(ids))


def upper_pairs(nblocks):
    pairs = [(j, k) for j in range(nblocks) for k in range(j, nblocks)]
    return pairs[:len(pairs) // 2], pairs[len(pairs) // 2:]


def gram_blocks(core_ref, parts_ref, local_ref, applied_ref, own_ref, other_ref):
    n = own_ref.shape[1]
    applied = local_ref[...]
    for i in range(parts_ref.shape[0]):
        applied = applied + parts_ref[i]
    applied_ref[...] = applied
    nblocks = applied.shape[1] // n
    rows = [dot_full(applied[:, j * n:(j + 1) * n], applied[:, j * n:], 0, 0) for j in range(nblocks)]
    for core in (0, 1):
        @pl.when(core_ref[0] == core)
        def _():
            for half, pairs in enumerate(upper_pairs(nblocks)):
                target = own_ref if half == core else other_ref
                for at, (j, k) in enumerate(pairs):
                    target[at] = rows[j][:, (k - j) * n:(k - j + 1) * n]


def three_parts(value):
    high = value.astype(jnp.bfloat16)
    rest = value - high.astype(jnp.float32)
    middle = rest.astype(jnp.bfloat16)
    return high, middle, (rest - middle.astype(jnp.float32)).astype(jnp.bfloat16)


def dot_few_rows(left, right):
    h, m, l = three_parts(left)
    high, middle, low = three_parts(right)
    stacked = jnp.concatenate([h, h, m, h, m, l]), jnp.concatenate([high, middle, high, low, middle, high])
    return lax.dot_general(*stacked, (((0,), (0,)), ((), ())), preferred_element_type=jnp.float32)


def factor_diagonal(a_ref, inverse_ref, u_ref, base, n):
    sub = lax.broadcasted_iota(jnp.int32, (STRIP, n), 0)
    lane = lax.broadcasted_iota(jnp.int32, (STRIP, n), 1)
    strips = n // STRIP

    def spread(rows, k):
        return jnp.broadcast_to(rows[k:k + 1, :], (STRIP, n))

    rows_a = [a_ref[STRIP * i:STRIP * (i + 1), :] for i in range(strips)]
    rows_e = [jnp.where(lane == sub + STRIP * i, 1.0, 0.0) for i in range(strips)]
    for s in range(strips):
        first = STRIP * s
        here = slice(first, first + STRIP)
        cols = [jnp.broadcast_to(rows_a[s][:, first + k:first + k + 1], (STRIP, n)) for k in range(STRIP)]
        down_a, down_e = rows_a[s], rows_e[s]
        full_a, full_e = rows_a[s], rows_e[s]
        pivots = None
        for k in range(STRIP):
            pivot = spread(cols[k], k)
            recip = 1.0 / pivot
            at = sub == k
            both = jnp.where(at, -1.0, cols[k]) * recip
            below = jnp.where(sub > k, cols[k], 0.0) * recip
            for b in range(k + 1, STRIP):
                cols[b] = jnp.where(at, 0.0, cols[b]) - both * spread(cols[b], k)
            row_a, row_e = spread(full_a, k), spread(full_e, k)
            down_a = down_a - below * spread(down_a, k)
            down_e = down_e - below * spread(down_e, k)
            full_a = jnp.where(at, 0.0, full_a) - both * row_a
            full_e = jnp.where(at, 0.0, full_e) - both * row_e
            pivots = pivot if pivots is None else jnp.where(sub >= k, pivot, pivots)
        scale = lax.rsqrt(pivots)
        u_ref[base + first:base + first + STRIP, base:base + n] = jnp.where(lane >= sub + first, down_a * scale, 0.0)
        inverse_ref[here, :] = down_e * scale
        if s + 1 < strips:
            here_a = rows_a[s]
            for k in range(STRIP):
                c = jnp.broadcast_to(rows_a[s + 1][:, first + k:first + k + 1], (STRIP, n))
                taken_a = c * spread(full_a, k) + (taken_a if k else 0.0)
                taken_e = c * spread(full_e, k) + (taken_e if k else 0.0)
            rows_a[s + 1], rows_e[s + 1] = rows_a[s + 1] - taken_a, rows_e[s + 1] - taken_e
        if s + 2 < strips:
            taken = dot_few_rows(here_a, jnp.concatenate([full_a, full_e], axis=1))
            for i in range(s + 2, strips):
                rows_a[i] = rows_a[i] - taken[STRIP * i:STRIP * (i + 1), :n]
                rows_e[i] = rows_e[i] - taken[STRIP * i:STRIP * (i + 1), n:]


def factor_and_solve(gram_ref, applied_ref, states_ref, u_ref, work, inverse):
    n = gram_ref.shape[1]
    size = u_ref.shape[0]
    nblocks = size // n
    for at, (j, k) in enumerate(sum(upper_pairs(nblocks), [])):
        work[n * j:n * (j + 1), n * k:n * (k + 1)] = gram_ref[at]
    states_ref[...] = applied_ref[...]
    u_ref[...] = jnp.zeros_like(u_ref)
    for j in range(nblocks):
        lo, hi = n * j, n * (j + 1)
        factor_diagonal(work.at[lo:hi, lo:hi], inverse, u_ref, lo, n)
        inv = inverse[...]
        solved = dot_full(states_ref[:, lo:hi], inv, 1, 1)
        states_ref[:, lo:hi] = solved
        if hi < size:
            panel = dot_full(inv, work[lo:hi, hi:], 1, 0)
            u_ref[lo:hi, hi:] = panel
            for k in range(j + 1, nblocks):
                a, b = n * k, n * (k + 1)
                work[a:b, a:] -= dot_full(panel[:, a - hi:b - hi], panel[:, a - hi:], 0, 0)
            states_ref[:, hi:] -= dot_full(solved, panel, 1, 0)


def call(body, outs, in_spaces, scratch=(), mib=40):
    return pl.pallas_call(
        body,
        out_shape=outs,
        in_specs=[pl.BlockSpec(memory_space=space) for space in in_spaces],
        out_specs=[pl.BlockSpec(memory_space=pltpu.VMEM) for _ in outs],
        scratch_shapes=list(scratch),
        compiler_params=pltpu.CompilerParams(vmem_limit_bytes=mib * 2**20),
    )


def line_places(ny, nz, nk):
    lines = []
    for fixed in range(ny):
        for k in range(nk):
            line = []
            for along in range(nz):
                y, z = (fixed, along) if k == 0 else (along, fixed)
                line.append((y * nz + z) * nk + k)
            lines.append(line)
    return lines


def ring_pairs(ny, nz, nk, step):
    pairs = []
    for y in range(ny):
        for z in range(nz):
            for k in range(nk):
                to_y, to_z = ((y + step) % ny, z) if k == 0 else (y, (z + step) % nz)
                pairs.append(((y * nz + z) * nk + k, (to_y * nz + to_z) * nk + k))
    return pairs


def gather_states(vectors):
    axes = ("y", "z", "k")
    sizes = tuple(lax.axis_size(axis) for axis in axes)
    copies = jnp.broadcast_to(vectors[None], (sizes[1],) + vectors.shape)
    line = lax.all_to_all(copies, axes, 0, 0, axis_index_groups=line_places(*sizes), tiled=True)
    half = line.shape[0] // 2
    up, down = ring_pairs(*sizes, 1), ring_pairs(*sizes, -1)
    halves = [line[:half], line[half:]]
    above, below = [[h] for h in halves], [[h] for h in halves]
    for step in range(4):
        for at in (0, 1):
            if step < 3 or at == 0:
                above[at].append(lax.ppermute(above[at][-1], axes, up))
            if step < 3 or at == 1:
                below[at].append(lax.ppermute(below[at][-1], axes, down))
    return above[0] + below[0][:0:-1] + above[1] + below[1][:0:-1]


def where_blocks(cols, y, z, k):
    from_y, from_z = cols // 8, cols % 8
    near = jnp.where(k == 0, from_z, from_y)
    far = jnp.where(k == 0, y - from_y, z - from_z) % 8
    return near // 4 * 8 + far, near % 4


def sum_groups(ny, nz, nx, nk):
    def device(y, z, x, k):
        return ((y * nz + z) * nx + x) * nk + k

    four, same = [], []
    for y in range(ny):
        for z in range(nz):
            four.append([device(y, z, x, 0) for x in range(nx)])
    for x in range(nx):
        same.append([device(y, z, x, 0) for y in range(ny) for z in range(nz)])
        for y in range(0, ny, 2):
            for z in range(0, nz, 2):
                four.append([device(y + i, z + j, x, 1) for i in (0, 1) for j in (0, 1)])
    for i in (0, 1):
        for j in (0, 1):
            same.append([
                device(y + i, z + j, x, 1)
                for x in range(nx) for y in range(0, ny, 2) for z in range(0, nz, 2)
            ])
    return four, same


def sum_halves(value):
    axes = ("y", "z", "x", "k")
    four, same = sum_groups(*(lax.axis_size(axis) for axis in axes))

    def exchange(pieces, groups):
        return lax.all_to_all(pieces, axes, 0, 0, axis_index_groups=groups, tiled=True)

    def copies(piece, groups):
        return jnp.broadcast_to(piece[None], (len(groups[0]),) + piece.shape)

    fours = len(four[0])
    every = [sum(same[:fours], []), sum(same[fours:], [])]
    piece = exchange(value.reshape(len(every[0]), -1), every).sum(0)
    part = exchange(copies(piece, same), same).reshape(-1, value.shape[-1])
    return exchange(copies(part, four), four).reshape(value.shape)


def per_device(vectors, onsite, tile_values, tile_rows, tile_cols, tile_count):
    own_rows, kstates = vectors.shape
    width = tile_values.shape[-1]
    slots = tile_values.shape[2]
    f32 = jnp.float32
    vm, sm = pltpu.VMEM, pltpu.SMEM
    halves = lax.axis_size("x")
    y, z, k = (lax.axis_index(axis) for axis in ("y", "z", "k"))

    rows = tile_rows.reshape(slots)
    source, place = where_blocks(tile_cols.reshape(slots), y, z, k)
    meta = jnp.concatenate([(rows + k) % 2 * halves + rows // 2, source, place, tile_count.reshape(1)])
    local = onsite[:, None] * vectors.astype(f32)
    buffers = gather_states(vectors)

    tiles = tile_values[0, 0]
    late = [4, 5, 11, 12]
    early = [at for at in range(len(buffers)) if at not in late]

    def products(ids, first_place, places, *base):
        return call(
            functools.partial(tile_products, ids, first_place, bool(base)),
            [jax.ShapeDtypeStruct((places, width, kstates), f32)],
            [sm, vm] + [vm] * (len(ids) + len(base)),
            (),
            24,
        )(meta, tiles, *[buffers[at] for at in ids], *base)[0]

    sums = products(early, 0, 2 * halves)
    send = products(late, halves, halves, sums)
    other = lax.ppermute(send, "k", [(0, 1), (1, 0)])
    keep = products(late, 0, halves, sums)
    parts = lax.all_to_all(keep + other, "x", 0, 0, tiled=True)

    nblocks = kstates // width
    half = jax.ShapeDtypeStruct((nblocks * (nblocks + 1) // 4, width, width), f32)
    applied, own, other = call(
        gram_blocks,
        [jax.ShapeDtypeStruct((own_rows, kstates), f32), half, half],
        [sm, vm, vm],
    )(k.astype(jnp.int32).reshape(1), parts, local)
    others = lax.all_gather(other, "k", axis=0)
    own = sum_halves(own + lax.dynamic_index_in_dim(others, 1 - k, 0, keepdims=False))
    gram = lax.all_gather(own, "k", axis=0, tiled=True)

    states, upper = call(
        factor_and_solve,
        [jax.ShapeDtypeStruct((own_rows, kstates), f32), jax.ShapeDtypeStruct((kstates, kstates), f32)],
        [vm, vm],
        [vm((kstates, kstates), f32), vm((width, width), f32)],
    )(gram, applied)
    return (states, upper)


def solution(mesh):
    fine = Mesh(mesh.devices.reshape(8, 8, 4, 2), ("y", "z", "x", "k"))
    row, col = ("y", "z"), ("x", "k")
    return jax.shard_map(
        per_device,
        mesh=fine,
        in_specs=(
            P(row + col, None),
            P(row + col),
            P(row, col, None, None, None),
            P(row, col, None),
            P(row, col, None),
            P(row, col),
        ),
        out_specs=(P(row + col, None), P()),
        check_vma=False,
    )
```

```python
import functools

import jax
import jax.numpy as jnp
from jax import lax
from jax.experimental import pallas as pl
from jax.experimental.pallas import tpu as pltpu
from jax.sharding import Mesh, PartitionSpec as P

FULL = lax.Precision.HIGHEST
STRIP = 16


def dot_full(left, right, left_dim, right_dim):
    dims = (((left_dim,), (right_dim,)), ((), ()))
    return lax.dot_general(left, right, dims, precision=FULL, preferred_element_type=jnp.float32)


def tile_products(ids, first_place, based, meta_ref, tiles_ref, *refs):
    sources, out_ref = refs[:len(ids)], refs[-1]
    slots, places = tiles_ref.shape[0], out_ref.shape[0]
    if based:
        out_ref[...] = refs[-2][first_place:first_place + places]
    else:
        out_ref[...] = jnp.zeros_like(out_ref)

    def add(t, place, which, first, last):
        if last - first == 1:
            @pl.when(which == ids[first])
            def _():
                block = sources[first][meta_ref[2 * slots + t]]
                out_ref[place] += jnp.dot(tiles_ref[t], block, preferred_element_type=jnp.float32)
            return
        middle = (first + last) // 2
        pl.when(which < ids[middle])(lambda: add(t, place, which, first, middle))
        pl.when(which >= ids[middle])(lambda: add(t, place, which, middle, last))

    @pl.loop(0, meta_ref[3 * slots])
    def _(t):
        place = meta_ref[t] - first_place

        @pl.when((place >= 0) & (place < places))
        def _():
            add(t, place, meta_ref[slots + t], 0, len(ids))


def upper_pairs(nblocks):
    pairs = [(j, k) for j in range(nblocks) for k in range(j, nblocks)]
    return pairs[:len(pairs) // 2], pairs[len(pairs) // 2:]


def gram_blocks(core_ref, parts_ref, local_ref, applied_ref, own_ref, other_ref):
    n = own_ref.shape[1]
    applied = local_ref[...]
    for i in range(parts_ref.shape[0]):
        applied = applied + parts_ref[i]
    applied_ref[...] = applied
    nblocks = applied.shape[1] // n
    rows = [dot_full(applied[:, j * n:(j + 1) * n], applied[:, j * n:], 0, 0) for j in range(nblocks)]
    for core in (0, 1):
        @pl.when(core_ref[0] == core)
        def _():
            for half, pairs in enumerate(upper_pairs(nblocks)):
                target = own_ref if half == core else other_ref
                for at, (j, k) in enumerate(pairs):
                    target[at] = rows[j][:, (k - j) * n:(k - j + 1) * n]


def three_parts(value):
    high = value.astype(jnp.bfloat16)
    rest = value - high.astype(jnp.float32)
    middle = rest.astype(jnp.bfloat16)
    return high, middle, (rest - middle.astype(jnp.float32)).astype(jnp.bfloat16)


def dot_few_rows(left, right):
    h, m, l = three_parts(left)
    high, middle, low = three_parts(right)
    stacked = jnp.concatenate([h, h, m, h, m, l]), jnp.concatenate([high, middle, high, low, middle, high])
    return lax.dot_general(*stacked, (((0,), (0,)), ((), ())), preferred_element_type=jnp.float32)


def factor_diagonal(a_ref, inverse_ref, u_ref, base, n):
    sub = lax.broadcasted_iota(jnp.int32, (STRIP, n), 0)
    lane = lax.broadcasted_iota(jnp.int32, (STRIP, n), 1)
    strips = n // STRIP

    def spread(rows, k):
        return jnp.broadcast_to(rows[k:k + 1, :], (STRIP, n))

    rows_a = [a_ref[STRIP * i:STRIP * (i + 1), :] for i in range(strips)]
    rows_e = [jnp.where(lane == sub + STRIP * i, 1.0, 0.0) for i in range(strips)]
    for s in range(strips):
        first = STRIP * s
        here = slice(first, first + STRIP)
        cols = [jnp.broadcast_to(rows_a[s][:, first + k:first + k + 1], (STRIP, n)) for k in range(STRIP)]
        down_a, down_e = rows_a[s], rows_e[s]
        full_a, full_e = rows_a[s], rows_e[s]
        pivots = None
        for k in range(STRIP):
            pivot = spread(cols[k], k)
            recip = 1.0 / pivot
            at = sub == k
            both = jnp.where(at, -1.0, cols[k]) * recip
            below = jnp.where(sub > k, cols[k], 0.0) * recip
            for b in range(k + 1, STRIP):
                cols[b] = jnp.where(at, 0.0, cols[b]) - both * spread(cols[b], k)
            row_a, row_e = spread(full_a, k), spread(full_e, k)
            down_a = down_a - below * spread(down_a, k)
            down_e = down_e - below * spread(down_e, k)
            full_a = jnp.where(at, 0.0, full_a) - both * row_a
            full_e = jnp.where(at, 0.0, full_e) - both * row_e
            pivots = pivot if pivots is None else jnp.where(sub >= k, pivot, pivots)
        scale = lax.rsqrt(pivots)
        u_ref[base + first:base + first + STRIP, base:base + n] = jnp.where(lane >= sub + first, down_a * scale, 0.0)
        inverse_ref[here, :] = down_e * scale
        if s + 1 < strips:
            here_a = rows_a[s]
            for k in range(STRIP):
                c = jnp.broadcast_to(rows_a[s + 1][:, first + k:first + k + 1], (STRIP, n))
                taken_a = c * spread(full_a, k) + (taken_a if k else 0.0)
                taken_e = c * spread(full_e, k) + (taken_e if k else 0.0)
            rows_a[s + 1], rows_e[s + 1] = rows_a[s + 1] - taken_a, rows_e[s + 1] - taken_e
        if s + 2 < strips:
            taken = dot_few_rows(here_a, jnp.concatenate([full_a, full_e], axis=1))
            for i in range(s + 2, strips):
                rows_a[i] = rows_a[i] - taken[STRIP * i:STRIP * (i + 1), :n]
                rows_e[i] = rows_e[i] - taken[STRIP * i:STRIP * (i + 1), n:]


def factor_and_solve(gram_ref, applied_ref, states_ref, u_ref, work, inverse):
    n = gram_ref.shape[1]
    size = u_ref.shape[0]
    nblocks = size // n
    for at, (j, k) in enumerate(sum(upper_pairs(nblocks), [])):
        work[n * j:n * (j + 1), n * k:n * (k + 1)] = gram_ref[at]
    states_ref[...] = applied_ref[...]
    u_ref[...] = jnp.zeros_like(u_ref)
    for j in range(nblocks):
        lo, hi = n * j, n * (j + 1)
        factor_diagonal(work.at[lo:hi, lo:hi], inverse, u_ref, lo, n)
        inv = inverse[...]
        solved = dot_full(states_ref[:, lo:hi], inv, 1, 1)
        states_ref[:, lo:hi] = solved
        if hi < size:
            panel = dot_full(inv, work[lo:hi, hi:], 1, 0)
            u_ref[lo:hi, hi:] = panel
            for k in range(j + 1, nblocks):
                a, b = n * k, n * (k + 1)
                work[a:b, a:] -= dot_full(panel[:, a - hi:b - hi], panel[:, a - hi:], 0, 0)
            states_ref[:, hi:] -= dot_full(solved, panel, 1, 0)


def call(body, outs, in_spaces, scratch=(), mib=40):
    return pl.pallas_call(
        body,
        out_shape=outs,
        in_specs=[pl.BlockSpec(memory_space=space) for space in in_spaces],
        out_specs=[pl.BlockSpec(memory_space=pltpu.VMEM) for _ in outs],
        scratch_shapes=list(scratch),
        compiler_params=pltpu.CompilerParams(vmem_limit_bytes=mib * 2**20),
    )


def line_places(ny, nz, nk):
    lines = []
    for fixed in range(ny):
        for k in range(nk):
            line = []
            for along in range(nz):
                y, z = (fixed, along) if k == 0 else (along, fixed)
                line.append((y * nz + z) * nk + k)
            lines.append(line)
    return lines


def ring_pairs(ny, nz, nk, step):
    pairs = []
    for y in range(ny):
        for z in range(nz):
            for k in range(nk):
                to_y, to_z = ((y + step) % ny, z) if k == 0 else (y, (z + step) % nz)
                pairs.append(((y * nz + z) * nk + k, (to_y * nz + to_z) * nk + k))
    return pairs


def gather_states(vectors):
    axes = ("y", "z", "k")
    sizes = tuple(lax.axis_size(axis) for axis in axes)
    copies = jnp.broadcast_to(vectors[None], (sizes[1],) + vectors.shape)
    line = lax.all_to_all(copies, axes, 0, 0, axis_index_groups=line_places(*sizes), tiled=True)
    half = line.shape[0] // 2
    up, down = ring_pairs(*sizes, 1), ring_pairs(*sizes, -1)
    halves = [line[:half], line[half:]]
    above, below = [[h] for h in halves], [[h] for h in halves]
    for step in range(4):
        for at in (0, 1):
            if step < 3 or at == 0:
                above[at].append(lax.ppermute(above[at][-1], axes, up))
            if step < 3 or at == 1:
                below[at].append(lax.ppermute(below[at][-1], axes, down))
    return above[0] + below[0][:0:-1] + above[1] + below[1][:0:-1]


def where_blocks(cols, y, z, k):
    from_y, from_z = cols // 8, cols % 8
    near = jnp.where(k == 0, from_z, from_y)
    far = jnp.where(k == 0, y - from_y, z - from_z) % 8
    return near // 4 * 8 + far, near % 4


def sum_groups(ny, nz, nx, nk):
    def device(y, z, x, k):
        return ((y * nz + z) * nx + x) * nk + k

    four, same = [], []
    for y in range(ny):
        for z in range(nz):
            four.append([device(y, z, x, 0) for x in range(nx)])
    for x in range(nx):
        same.append([device(y, z, x, 0) for y in range(ny) for z in range(nz)])
        for y in range(0, ny, 2):
            for z in range(0, nz, 2):
                four.append([device(y + i, z + j, x, 1) for i in (0, 1) for j in (0, 1)])
    for i in (0, 1):
        for j in (0, 1):
            same.append([
                device(y + i, z + j, x, 1)
                for x in range(nx) for y in range(0, ny, 2) for z in range(0, nz, 2)
            ])
    return four, same


def sum_halves(value):
    axes = ("y", "z", "x", "k")
    four, same = sum_groups(*(lax.axis_size(axis) for axis in axes))

    def exchange(pieces, groups):
        return lax.all_to_all(pieces, axes, 0, 0, axis_index_groups=groups, tiled=True)

    def copies(piece, groups):
        return jnp.broadcast_to(piece[None], (len(groups[0]),) + piece.shape)

    part = exchange(value.reshape(len(four[0]), -1, value.shape[-1]), four).sum(0)
    piece = exchange(part.reshape(len(same[0]), -1), same).sum(0)
    part = exchange(copies(piece, same), same).reshape(part.shape)
    return exchange(copies(part, four), four).reshape(value.shape)


def per_device(vectors, onsite, tile_values, tile_rows, tile_cols, tile_count):
    own_rows, kstates = vectors.shape
    width = tile_values.shape[-1]
    slots = tile_values.shape[2]
    f32 = jnp.float32
    vm, sm = pltpu.VMEM, pltpu.SMEM
    halves = lax.axis_size("x")
    y, z, k = (lax.axis_index(axis) for axis in ("y", "z", "k"))

    rows = tile_rows.reshape(slots)
    source, place = where_blocks(tile_cols.reshape(slots), y, z, k)
    meta = jnp.concatenate([(rows + k) % 2 * halves + rows // 2, source, place, tile_count.reshape(1)])
    local = onsite[:, None] * vectors.astype(f32)
    buffers = gather_states(vectors)

    tiles = tile_values[0, 0]
    late = [4, 5, 11, 12]
    early = [at for at in range(len(buffers)) if at not in late]

    def products(ids, first_place, places, *base):
        return call(
            functools.partial(tile_products, ids, first_place, bool(base)),
            [jax.ShapeDtypeStruct((places, width, kstates), f32)],
            [sm, vm] + [vm] * (len(ids) + len(base)),
            (),
            24,
        )(meta, tiles, *[buffers[at] for at in ids], *base)[0]

    sums = products(early, 0, 2 * halves)
    send = products(late, halves, halves, sums)
    other = lax.ppermute(send, "k", [(0, 1), (1, 0)])
    keep = products(late, 0, halves, sums)
    parts = lax.all_to_all(keep + other, "x", 0, 0, tiled=True)

    nblocks = kstates // width
    half = jax.ShapeDtypeStruct((nblocks * (nblocks + 1) // 4, width, width), f32)
    applied, own, other = call(
        gram_blocks,
        [jax.ShapeDtypeStruct((own_rows, kstates), f32), half, half],
        [sm, vm, vm],
    )(k.astype(jnp.int32).reshape(1), parts, local)
    others = lax.all_gather(other, "k", axis=0)
    own = sum_halves(own + lax.dynamic_index_in_dim(others, 1 - k, 0, keepdims=False))
    gram = lax.all_gather(own, "k", axis=0, tiled=True)

    states, upper = call(
        factor_and_solve,
        [jax.ShapeDtypeStruct((own_rows, kstates), f32), jax.ShapeDtypeStruct((kstates, kstates), f32)],
        [vm, vm],
        [vm((kstates, kstates), f32), vm((width, width), f32)],
    )(gram, applied)
    return (states, upper)


def solution(mesh):
    fine = Mesh(mesh.devices.reshape(8, 8, 4, 2), ("y", "z", "x", "k"))
    row, col = ("y", "z"), ("x", "k")
    return jax.shard_map(
        per_device,
        mesh=fine,
        in_specs=(
            P(row + col, None),
            P(row + col),
            P(row, col, None, None, None),
            P(row, col, None),
            P(row, col, None),
            P(row, col),
        ),
        out_specs=(P(row + col, None), P()),
        check_vma=False,
    )
```
